256 devices in a mesh: dp: 4 (over x_lo, core), expert: 64 (over z, y, x_hi).
Axes of the slice: x: 4 (x_hi: 2, x_lo: 2; x = x_hi * 2 + x_lo), y: 4, z: 8, core: 2. Of those that a mesh axis runs over, the one named last changes fastest.
Arguments:
- tokens: bfloat16 [40960, 2048], P(('dp', 'expert')), may hold values from -6 to 6
- routes: int32 [40960, 2], P(('dp', 'expert')), may hold values from 0 to 63, all different within a row
- gate_probs: float32 [40960, 2], P(('dp', 'expert')), may hold values from 0.1 to 1
- cotangent: bfloat16 [40960, 2048], P(('dp', 'expert')), may hold values from -6 to 6
- w_gate: bfloat16 [64, 2048, 768], P('expert', 'dp'), may hold values from -0.125 to 0.125
- w_up: bfloat16 [64, 2048, 768], P('expert', 'dp'), may hold values from -0.125 to 0.125
- w_down: bfloat16 [64, 768, 2048], P('expert', None, 'dp'), may hold values from -0.21875 to 0.21875
Outputs:
- layer_out: bfloat16 [40960, 2048], P(('dp', 'expert'))
- d_tokens: bfloat16 [40960, 2048], P(('dp', 'expert'))
- d_gates: float32 [40960, 2], P(('dp', 'expert'))
- grad_gate: float32 [64, 2048, 768], P('expert', 'dp')
- grad_up: float32 [64, 2048, 768], P('expert', 'dp')
- grad_down: float32 [64, 768, 2048], P('expert', None, 'dp')
The draws below stay inside these ranges and needn't reach their ends.
Inputs may be any that keep to these rules, and one draw needn't show every extreme that they name: `routes`: each row names 2 different experts; every expert is named by some row.
All inputs are finite; a program needn't handle non-finite values.
Results may differ from the reference program's by a relative error of at most 0.0065.
Values may be sent and summed in bfloat16 or wider, within the bound.
A program may use at most 128 MiB of HBM per device.

```python
import jax
import jax.numpy as jnp
from jax import lax

D = 2048
FF = 768
ROUTES = 2
TOK_DEV = 160
EXPERTS = 64
CAP = 7
TOKENS = 40960


def level_of(key, shape, split, least, largest):
    gain = 1.0
    for axis_at, parts in split:
        heights = jax.random.uniform(jax.random.fold_in(jax.random.fold_in(key, 6), axis_at), (parts,), jnp.float32, least / len(split), largest / len(split))
        gain = gain * jnp.repeat(jnp.exp(heights), shape[axis_at] // parts).reshape((-1,) + (1,) * (len(shape) - 1 - axis_at))
    return gain


def distinct(own_key, rows, number_of, top, lift):
    ranking = jax.random.permutation(jax.random.fold_in(own_key, 1), number_of)
    pull = ranking
    for power in range(3):
        pull = pull * pull // number_of
    pull = pull * lift // number_of
    tickets = jax.random.randint(jax.random.fold_in(own_key, 2), (rows, number_of), 0, 4096) + pull
    holders = jax.random.permutation(jax.random.fold_in(own_key, 3), rows)[jnp.arange(number_of) % rows]
    tickets = jnp.where(jnp.arange(rows)[:, None] == holders[None, :], 1 << 14, tickets)
    priority = tickets * number_of + jnp.arange(number_of)
    return lax.top_k(priority.astype(jnp.int32), top)[1].astype(jnp.int32)


def centred(rng, extent, width, bound, pieces=(), kind=jnp.bfloat16):
    loudness = level_of(rng, extent, pieces, -0.22, 0.18) if pieces else 1.0
    values = jax.random.normal(rng, extent, jnp.float32) * width * loudness
    return jnp.minimum(jnp.maximum(values, -bound), bound).astype(kind)


def setup_inputs(seed: int = 0) -> dict:
    seeds = jax.random.split(jax.random.key(seed), 8)
    return {
        "tokens": centred(seeds[0], (TOKENS, D), 1.0, 6.0, ((0, 256),)),
        "routes": distinct(seeds[1], TOKENS, EXPERTS, ROUTES, 256),
        "gate_probs": jnp.clip(0.1 + 0.9 * jax.random.uniform(seeds[2], (TOKENS, ROUTES), jnp.float32) ** level_of(seeds[2], (TOKENS, ROUTES), ((0, 256),), -0.2, 0.2), 0.1, 1.0),
        "cotangent": centred(seeds[3], (TOKENS, D), 1.0, 6.0, ((0, 256),)),
        "w_gate": centred(seeds[4], (EXPERTS, D, FF), D ** -0.5, 0.125, ((0, 64), (1, 4))),
        "w_up": centred(seeds[5], (EXPERTS, D, FF), D ** -0.5, 0.125, ((0, 64), (1, 4))),
        "w_down": centred(seeds[6], (EXPERTS, FF, D), FF ** -0.5, 0.21875, ((0, 64), (2, 4))),
    }


def silu_parts(pre_act):
    sig_value = jax.nn.sigmoid(pre_act)
    return pre_act * sig_value, sig_value * (1.0 + pre_act * (1.0 - sig_value))


def contract_rows(first_op, second_op):
    return lax.dot_general(first_op, second_op, (((0,), (0,)), ((), ())), preferred_element_type=jnp.float32)


def contract_last(first_op, second_op):
    return lax.dot_general(first_op, second_op, (((1,), (1,)), ((), ())), preferred_element_type=jnp.float32)


def expert_forward(flat_rows, weights):
    gate_mat, up_mat, down_mat = weights
    gate_pre = jnp.dot(flat_rows, gate_mat, preferred_element_type=jnp.float32)
    up_pre = jnp.dot(flat_rows, up_mat, preferred_element_type=jnp.float32)
    active, unused_slope = silu_parts(gate_pre)
    hidden = (active * up_pre).astype(jnp.bfloat16)
    result = jnp.dot(hidden, down_mat, preferred_element_type=jnp.float32).astype(jnp.bfloat16)
    return gate_pre, up_pre, hidden, result


def expert_backward(route_grad, gate_pre, up_pre, weights):
    gate_mat, up_mat, down_mat = weights
    d_hidden = contract_last(route_grad, down_mat)
    active, silu_slope = silu_parts(gate_pre)
    d_gate = (d_hidden * up_pre * silu_slope).astype(jnp.bfloat16)
    d_up = (d_hidden * active).astype(jnp.bfloat16)
    d_rows = (contract_last(d_gate, gate_mat) + contract_last(d_up, up_mat)).astype(jnp.bfloat16)
    return d_gate, d_up, d_rows


def reference(tokens, routes, gate_probs, cotangent, w_gate, w_up, w_down):
    experts = w_gate.shape[0]
    blocks = tokens.shape[0] // TOK_DEV
    token_rows = tokens.reshape(blocks, TOK_DEV, D)
    grad_rows = cotangent.reshape(blocks, TOK_DEV, D)
    route_ids = routes.reshape(blocks, TOK_DEV, ROUTES)
    probs = gate_probs.reshape(blocks, TOK_DEV, ROUTES)
    expert_hits = (route_ids[..., None] == jnp.arange(experts, dtype=jnp.int32)).astype(jnp.int32).sum(2)
    before = jnp.cumsum(expert_hits, axis=1) - expert_hits
    slot_rank = jnp.take_along_axis(before, route_ids, axis=2)
    is_kept = slot_rank < CAP
    block_ids = jnp.broadcast_to(jnp.arange(blocks, dtype=jnp.int32)[:, None, None], route_ids.shape)
    token_ids = jnp.broadcast_to(jnp.arange(TOK_DEV, dtype=jnp.int32)[None, :, None], route_ids.shape)
    safe_rank = jnp.where(is_kept, slot_rank, CAP).astype(jnp.int32)
    table = jnp.full((blocks, experts, CAP), TOK_DEV, jnp.int32)
    table = table.at[block_ids, route_ids, safe_rank].set(token_ids, mode="drop")
    slot_probs = jnp.zeros((blocks, experts, CAP), jnp.float32)
    slot_probs = slot_probs.at[block_ids, route_ids, safe_rank].set(probs, mode="drop")
    pad_tokens = jnp.concatenate([token_rows, jnp.zeros((blocks, 1, D), token_rows.dtype)], 1)
    pad_grads = jnp.concatenate([grad_rows, jnp.zeros((blocks, 1, D), grad_rows.dtype)], 1)
    block_col = jnp.arange(blocks, dtype=jnp.int32)[:, None]

    def one_expert(carry, inputs):
        out_sum, dx_sum, gate_grad = carry
        expert, gate_mat, up_mat, down_mat, where_rows, where_probs = inputs
        gathered = pad_tokens[block_col, where_rows]
        incoming = pad_grads[block_col, where_rows]
        flat_rows = gathered.reshape(-1, D)
        weights = (gate_mat, up_mat, down_mat)
        gate_pre, up_pre, hidden, result = expert_forward(flat_rows, weights)
        route_grad = (where_probs.reshape(-1, 1) * incoming.reshape(-1, D).astype(jnp.float32)).astype(jnp.bfloat16)
        d_gate, d_up, d_rows = expert_backward(route_grad, gate_pre, up_pre, weights)
        grads = (contract_rows(flat_rows, d_gate), contract_rows(flat_rows, d_up), contract_rows(hidden, route_grad))
        result_wide = result.astype(jnp.float32).reshape(blocks, CAP, D)
        out_sum = out_sum.at[block_col, where_rows].add(where_probs[..., None] * result_wide)
        dx_sum = dx_sum.at[block_col, where_rows].add(d_rows.astype(jnp.float32).reshape(blocks, CAP, D))
        slot_dot = jnp.sum(incoming.astype(jnp.float32) * result_wide, axis=-1)
        gate_grad = gate_grad.at[block_col, where_rows, expert].set(slot_dot)
        return (out_sum, dx_sum, gate_grad), grads

    start = (jnp.zeros((blocks, TOK_DEV + 1, D), jnp.float32),
             jnp.zeros((blocks, TOK_DEV + 1, D), jnp.float32),
             jnp.zeros((blocks, TOK_DEV + 1, experts), jnp.float32))
    inputs = (jnp.arange(experts, dtype=jnp.int32), w_gate, w_up, w_down,
              jnp.transpose(table, (1, 0, 2)), jnp.transpose(slot_probs, (1, 0, 2)))
    (out_sum, dx_sum, gate_grad), (grad_gate, grad_up, grad_down) = lax.scan(one_expert, start, inputs)
    layer_out = out_sum[:, :TOK_DEV].reshape(-1, D).astype(jnp.bfloat16)
    d_tokens = dx_sum[:, :TOK_DEV].reshape(-1, D).astype(jnp.bfloat16)
    d_gates = jnp.take_along_axis(gate_grad[:, :TOK_DEV], route_ids, axis=2).reshape(-1, ROUTES)
    return (layer_out, d_tokens, d_gates, grad_gate, grad_up, grad_down)
```

```python
import functools

import jax
import jax.numpy as jnp
from jax import lax
from jax.experimental import pallas as pl
from jax.experimental.pallas import tpu as pltpu
from jax.sharding import PartitionSpec as P

MESH = pl.DeviceIdType.MESH
LANE = 128
PLANE = 8
NY = 4
TILE = 256
F32 = jnp.float32
BF16 = jnp.bfloat16


def mm(a, b):
    return jnp.dot(a, b, preferred_element_type=F32)


def mm_last(a, b):
    return lax.dot_general(a, b, (((1,), (1,)), ((), ())), preferred_element_type=F32)


def mm_first(a, b):
    return lax.dot_general(a, b, (((0,), (0,)), ((), ())), preferred_element_type=F32)


def kernel(
    cap,
    tok, routes, probs, cot, wg_in, wu_in, wd_in,
    lay_o, dtok_o, dgate_o, gg_o, gu_o, gd_o,
    slot_s, rg, xs, gs, os_, xr, gr, orr, dxr, X, XT, HT, WG, WU, WD, A, B, HID, DG, DU, scr,
    sib_s, sib_r, sibd_s, sibd_r, crs_s, crs_r, crsd_s, crsd_r, fin, find,
    a2a_send, a2a_recv, a2a_loc, ag_loc, ag_send, ag_cross, ag_sib, ag_fwd_s, ag_fwd_r,
    sib_ss, sib_rs, crs_ss, crs_rs, out_sem,
):
    T, D = tok.shape
    E = lax.axis_size("expert")
    NZ = E // PLANE
    S = E * cap
    ROWS = D // LANE
    NP = WG.shape[0]
    PC = D // NP
    FF = WG.shape[2]
    CH = PLANE * cap
    dp = lax.axis_index("dp")
    me = lax.axis_index("expert")
    core, xlo = dp % 2, dp // 2
    sib_dp = 2 * xlo + (1 - core)
    crs_dp = 2 * (1 - xlo) + core
    sibling, across = (sib_dp, me), (crs_dp, me)
    my_z, my_y, my_x = me // PLANE, (me // 2) % NY, me % 2

    def partner(dz, i):
        dy, dx = i // 2, i % 2
        e = ((my_z + dz) % NZ) * PLANE + ((my_y + dy) % NY) * 2 + (my_x + dx) % 2
        return (dp + 2 * dx) % 4, e

    barrier = pltpu.get_barrier_semaphore()

    def greet(k, carry):
        pl.semaphore_signal(barrier, inc=1, device_id=partner(k // PLANE, k % PLANE), device_id_type=MESH)
        return carry

    lax.fori_loop(1, E, greet, 0)
    pl.semaphore_signal(barrier, inc=1, device_id=sibling, device_id_type=MESH)
    pl.semaphore_signal(barrier, inc=1, device_id=across, device_id_type=MESH)

    r0, r1 = routes[:, 0:1], routes[:, 1:2]
    iota_e = lax.broadcasted_iota(jnp.int32, (T, E), 1)
    h0, h1 = r0 == iota_e, r1 == iota_e
    hits = (jnp.where(h0, 1.0, 0.0) + jnp.where(h1, 1.0, 0.0)).astype(BF16)
    tri = jnp.where(
        lax.broadcasted_iota(jnp.int32, (T, T), 0) > lax.broadcasted_iota(jnp.int32, (T, T), 1), 1.0, 0.0
    ).astype(BF16)
    before = mm(tri, hits)
    for k, (r, h) in enumerate(((r0, h0), (r1, h1))):
        rank = jnp.sum(jnp.where(h, before, 0.0), axis=1, keepdims=True).astype(jnp.int32)
        slot_s[:, k : k + 1] = jnp.where(rank < cap, r * cap + rank, S)
        rg[k * T : (k + 1) * T, :] = (probs[:, k : k + 1] * cot[...].astype(F32)).astype(BF16)

    pl.semaphore_wait(barrier, E + 1)

    mats = ((wg_in, WG), (wu_in, WU), (wd_in, WD))
    ag = []
    for m, (src, full) in enumerate(mats):
        c = pltpu.make_async_remote_copy(
            src, full.at[dp], ag_send.at[m], ag_cross.at[m], device_id=across, device_id_type=MESH
        )
        c.start()
        s = pltpu.make_async_remote_copy(
            src, full.at[dp], ag_send.at[3 + m], ag_sib.at[m], device_id=sibling, device_id_type=MESH
        )
        s.start()
        l = pltpu.make_async_copy(src, full.at[dp], ag_loc.at[m])
        l.start()
        ag.append((c, s, l))

    def send_block(a, src, dst, dz, i):
        d, e = partner(dz, i)
        pltpu.make_async_remote_copy(
            src.at[pl.ds(e * cap, cap)],
            dst.at[pl.ds(me * cap, cap)],
            a2a_send.at[a],
            a2a_recv.at[a],
            device_id=(d, e),
            device_id_type=MESH,
        ).start()

    def exchange(a, fill, src, dst):
        def plane(q, carry):
            half = (q + 1) // 2
            dz = (NZ // 2 + half * (2 * (q % 2) - 1)) % NZ
            fill(((my_z + dz) % NZ) * CH)

            def one(i, c):
                send_block(a, src, dst, dz, i)
                return c

            lax.fori_loop(0, PLANE, one, 0)
            return carry

        lax.fori_loop(0, NZ - 1, plane, 0)
        fill(my_z * CH)
        mine = pl.ds(me * cap, cap)
        pltpu.make_async_copy(src.at[mine], dst.at[mine], a2a_loc.at[a]).start()

        def rest(i, c):
            send_block(a, src, dst, 0, i)
            return c

        lax.fori_loop(1, PLANE, rest, 0)

    def arrived(a, src, dst):
        block = dst.at[pl.ds(0, S - cap)]
        pltpu.make_async_copy(block, block, a2a_recv.at[a]).wait()
        mine = pl.ds(me * cap, cap)
        pltpu.make_async_copy(src.at[mine], dst.at[mine], a2a_loc.at[a]).wait()

    def sent(a, src):
        block = src.at[pl.ds(0, S - cap)]
        pltpu.make_async_copy(block, block, a2a_send.at[a]).wait()

    def lay_rows(v, dst, base):
        for j in range(ROWS):
            scr[pl.ds(j, CH, stride=ROWS), :] = v[:, j * LANE : (j + 1) * LANE]
        dst[pl.ds(base, CH)] = scr[pl.ds(0, CH * ROWS), :].reshape(CH, ROWS, LANE).astype(BF16)

    def onehot(k, base, n):
        return jnp.where(
            slot_s[:, k : k + 1] == lax.broadcasted_iota(jnp.int32, (T, n), 1) + base, 1.0, 0.0
        )

    def fill_x(base):
        pick = (onehot(0, base, CH) + onehot(1, base, CH)).astype(BF16)
        lay_rows(mm_first(pick, tok[...]), xs, base)

    def fill_g(base):
        v = mm_first(onehot(0, base, CH).astype(BF16), rg[0:T, :])
        v += mm_first(onehot(1, base, CH).astype(BF16), rg[T : 2 * T, :])
        lay_rows(v, gs, base)

    exchange(0, fill_x, xs, xr)
    exchange(1, fill_g, gs, gr)

    def forward_weights(m):
        full = mats[m][1]
        ag[m][0].wait_recv()
        f = pltpu.make_async_remote_copy(
            full.at[crs_dp], full.at[crs_dp], ag_fwd_s.at[m], ag_fwd_r.at[m], device_id=sibling, device_id_type=MESH
        )
        f.start()
        return f

    def weights_here(m, f):
        ag[m][2].wait()
        ag[m][1].wait_recv()
        f.wait_recv()

    def unpack(src):
        step = 16 * cap

        def chunk(c, carry):
            rows = pl.ds(pl.multiple_of(c * step, 16), step)
            scr[pl.ds(0, step * ROWS), :] = src[rows].astype(F32).reshape(step * ROWS, LANE)
            for j in range(ROWS):
                p, o = divmod(j * LANE, PC)
                X[p, rows, o : o + LANE] = scr[pl.ds(j, step, stride=ROWS), :].astype(BF16)
            return carry

        lax.fori_loop(0, S // step, chunk, 0)

    fwd = [forward_weights(0), forward_weights(1)]
    arrived(0, xs, xr)
    unpack(xr)
    weights_here(0, fwd[0])
    weights_here(1, fwd[1])

    def up_tile(n, carry):
        cols = pl.ds(pl.multiple_of(n * TILE, TILE), TILE)
        gate = mm(X[0], WG[0, :, cols])
        up = mm(X[0], WU[0, :, cols])
        for p in range(1, NP):
            gate += mm(X[p], WG[p, :, cols])
            up += mm(X[p], WU[p, :, cols])
        s = jax.nn.sigmoid(gate)
        act = gate * s
        A[:, cols] = up * (s * (1.0 + gate * (1.0 - s)))
        B[:, cols] = act
        HID[:, cols] = (act * up).astype(BF16)
        return carry

    lax.fori_loop(0, FF // TILE, up_tile, 0)
    fwd.append(forward_weights(2))
    weights_here(2, fwd[2])

    def rows_out(p, v):
        for j in range(PC // LANE):
            scr[pl.ds(p * (PC // LANE) + j, S, stride=ROWS), :] = v[:, j * LANE : (j + 1) * LANE]

    def fill_from_scr(dst):
        def fill(base):
            dst[pl.ds(base, CH)] = (
                scr[pl.ds(pl.multiple_of(base * ROWS, ROWS), CH * ROWS), :].reshape(CH, ROWS, LANE).astype(BF16)
            )

        return fill

    for p in range(NP):
        rows_out(p, mm(HID[...], WD[p]))
    exchange(2, fill_from_scr(os_), os_, orr)

    for p in range(NP):
        XT[p] = X[p].T
    HT[...] = HID[...].T

    arrived(1, gs, gr)
    unpack(gr)

    def to_sibling(k, buf_s, buf_r, s):
        c = pltpu.make_async_remote_copy(
            buf_s, buf_r, sib_ss.at[k, s], sib_rs.at[k, s], device_id=sibling, device_id_type=MESH
        )
        c.start()
        return c

    def to_across(k, buf_s, buf_r):
        c = pltpu.make_async_remote_copy(
            buf_s, buf_r, crs_ss.at[k], crs_rs.at[k], device_id=across, device_id_type=MESH
        )
        c.start()
        return c

    def part_down(p):
        return mm(HT[...], X[p])

    def part_gu(m, p):
        return mm(XT[p], (DG, DU)[m][...])

    sib = {}
    for s in range(2):
        sibd_s[s] = part_down(2 * s + (1 - core)).astype(BF16)
        sib[2, s] = to_sibling(2, sibd_s.at[s], sibd_r.at[s], s)

    def dh_tile(n, carry):
        cols = pl.ds(pl.multiple_of(n * TILE, TILE), TILE)
        dh = mm_last(X[0], WD[0, cols, :])
        for p in range(1, NP):
            dh += mm_last(X[p], WD[p, cols, :])
        DG[:, cols] = (dh * A[:, cols]).astype(BF16)
        DU[:, cols] = (dh * B[:, cols]).astype(BF16)
        return carry

    lax.fori_loop(0, FF // TILE, dh_tile, 0)
    for m in range(2):
        for s in range(2):
            sib_s[m, s] = part_gu(m, 2 * s + (1 - core)).astype(BF16)
            sib[m, s] = to_sibling(m, sib_s.at[m, s], sib_r.at[m, s], s)

    for s in range(2):
        sib[2, s].wait_recv()
    crsd_s[...] = (part_down(crs_dp) + sibd_r[1 - xlo].astype(F32)).astype(BF16)
    crs = [None, None, to_across(2, crsd_s, crsd_r)]
    for m in range(2):
        for s in range(2):
            sib[m, s].wait_recv()
        crs_s[m] = (part_gu(m, crs_dp) + sib_r[m, 1 - xlo].astype(F32)).astype(BF16)
        crs[m] = to_across(m, crs_s.at[m], crs_r.at[m])

    sent(0, xs)
    for p in range(NP):
        rows_out(p, mm_last(DG[...], WG[p]) + mm_last(DU[...], WU[p]))
    exchange(3, fill_from_scr(xs), xs, dxr)

    find[...] = part_down(dp) + sibd_r[xlo].astype(F32)
    for m in range(2):
        fin[m] = part_gu(m, dp) + sib_r[m, xlo].astype(F32)

    arrived(2, os_, orr)
    unpack(orr)
    p0, p1 = onehot(0, 0, S).astype(BF16), onehot(1, 0, S).astype(BF16)
    dg0 = jnp.zeros((T, 1), F32)
    dg1 = jnp.zeros((T, 1), F32)
    for p in range(NP):
        cols = slice(p * PC, (p + 1) * PC)
        k0, k1 = mm(p0, X[p]), mm(p1, X[p])
        lay_o[:, cols] = (probs[:, 0:1] * k0 + probs[:, 1:2] * k1).astype(BF16)
        c32 = cot[:, cols].astype(F32)
        dg0 += jnp.sum(c32 * k0, axis=1, keepdims=True)
        dg1 += jnp.sum(c32 * k1, axis=1, keepdims=True)
    dgate_o[:, 0:1] = dg0
    dgate_o[:, 1:2] = dg1

    outs = []
    crs[2].wait_recv()
    find[...] += crsd_r[...].astype(F32)
    outs.append(pltpu.make_async_copy(find, gd_o, out_sem.at[2]))
    outs[-1].start()
    for m, o in enumerate((gg_o, gu_o)):
        crs[m].wait_recv()
        fin[m] += crs_r[m].astype(F32)
        outs.append(pltpu.make_async_copy(fin.at[m], o, out_sem.at[m]))
        outs[-1].start()

    arrived(3, xs, dxr)
    unpack(dxr)
    both = p0 + p1
    for p in range(NP):
        dtok_o[:, p * PC : (p + 1) * PC] = mm(both, X[p]).astype(BF16)

    sent(1, gs)
    sent(2, os_)
    sent(3, xs)
    for m in range(3):
        ag[m][0].wait_send()
        ag[m][1].wait_send()
        fwd[m].wait_send()
        crs[m].wait_send()
        for s in range(2):
            sib[m, s].wait_send()
    for o in outs:
        o.wait()


def on_device(tokens, routes, gate_probs, cotangent, w_gate, w_up, w_down):
    T, D = tokens.shape
    E = lax.axis_size("expert")
    NP = lax.axis_size("dp")
    PC, FF = w_gate.shape[1:]
    cap = max(2, 3 * T * routes.shape[1] // (2 * E))
    S = E * cap
    ROWS = D // LANE
    slots = pltpu.VMEM((S, ROWS, LANE), BF16)
    dma = pltpu.SemaphoreType.DMA
    vmem = pl.BlockSpec(memory_space=pltpu.VMEM)
    hbm = pl.BlockSpec(memory_space=pl.ANY)
    scratch = [
        pltpu.VMEM((T, 2), jnp.int32),
        pltpu.VMEM((2 * T, D), BF16),
        *([slots] * 7),
        pltpu.VMEM((NP, S, PC), BF16),
        pltpu.VMEM((NP, PC, S), BF16),
        pltpu.VMEM((FF, S), BF16),
        pltpu.VMEM((NP, PC, FF), BF16),
        pltpu.VMEM((NP, PC, FF), BF16),
        pltpu.VMEM((NP, FF, PC), BF16),
        pltpu.VMEM((S, FF), F32),
        pltpu.VMEM((S, FF), F32),
        *([pltpu.VMEM((S, FF), BF16)] * 3),
        pltpu.VMEM((S * ROWS, LANE), F32),
        pltpu.VMEM((2, 2, PC, FF), BF16),
        pltpu.VMEM((2, 2, PC, FF), BF16),
        pltpu.VMEM((2, FF, PC), BF16),
        pltpu.VMEM((2, FF, PC), BF16),
        pltpu.VMEM((2, PC, FF), BF16),
        pltpu.VMEM((2, PC, FF), BF16),
        pltpu.VMEM((FF, PC), BF16),
        pltpu.VMEM((FF, PC), BF16),
        pltpu.VMEM((2, PC, FF), F32),
        pltpu.VMEM((FF, PC), F32),
        dma((4,)), dma((4,)), dma((4,)),
        dma((3,)), dma((6,)), dma((3,)), dma((3,)), dma((3,)), dma((3,)),
        dma((3, 2)), dma((3, 2)), dma((3,)), dma((3,)), dma((3,)),
    ]
    lay, dtok, dgates, gg, gu, gd = pl.pallas_call(
        functools.partial(kernel, cap),
        out_shape=(
            jax.ShapeDtypeStruct((T, D), BF16),
            jax.ShapeDtypeStruct((T, D), BF16),
            jax.ShapeDtypeStruct((T, 2), F32),
            jax.ShapeDtypeStruct((PC, FF), F32),
            jax.ShapeDtypeStruct((PC, FF), F32),
            jax.ShapeDtypeStruct((FF, PC), F32),
        ),
        in_specs=[vmem, vmem, vmem, vmem, hbm, hbm, hbm],
        out_specs=(vmem, vmem, vmem, hbm, hbm, hbm),
        scratch_shapes=scratch,
        compiler_params=pltpu.CompilerParams(
            collective_id=0, has_side_effects=True, vmem_limit_bytes=64000 * 1024
        ),
    )(tokens, routes, gate_probs, cotangent, w_gate[0], w_up[0], w_down[0])
    return lay, dtok, dgates, gg[None], gu[None], gd[None]


def solution(mesh):
    rows = P(("dp", "expert"), None)
    weights = (P("expert", "dp", None), P("expert", "dp", None), P("expert", None, "dp"))
    return jax.shard_map(
        on_device,
        mesh=mesh,
        in_specs=(rows, rows, rows, rows, *weights),
        out_specs=(rows, rows, rows, *weights),
        check_vma=False,
    )
```

```python
import functools

import jax
import jax.numpy as jnp
from jax import lax
from jax.experimental import pallas as pl
from jax.experimental.pallas import tpu as pltpu
from jax.sharding import PartitionSpec as P

MESH = pl.DeviceIdType.MESH
LANE = 128
PLANE = 8
NY = 4
TILE = 256
F32 = jnp.float32
BF16 = jnp.bfloat16


def mm(a, b):
    return jnp.dot(a, b, preferred_element_type=F32)


def mm_last(a, b):
    return lax.dot_general(a, b, (((1,), (1,)), ((), ())), preferred_element_type=F32)


def mm_first(a, b):
    return lax.dot_general(a, b, (((0,), (0,)), ((), ())), preferred_element_type=F32)


def kernel(
    cap,
    tok_in, routes_in, probs_in, cot_in, wg_in, wu_in, wd_in,
    lay_o, dgate_o, slot_o, dxr, gg_o, gu_o, gd_o,
    tok, routes, probs_t, cot, probs, lay, dgate, slot_s, rg, xs, gs, os_, xr, gr, orr, X, XT, HT, WG, WU, WD, A, B, HID, DG, DU, scr,
    sib_s, sib_r, sibd_s, sibd_r, crs_s, crs_r, crsd_s, crsd_r, fin, find,
    a2a_send, a2a_recv, a2a_loc, ag_loc, ag_send, ag_cross, ag_sib, ag_fwd_s, ag_fwd_r,
    sib_ss, sib_rs, crs_ss, crs_rs, in_sem, out_sem,
):
    T, D = tok.shape
    E = lax.axis_size("expert")
    NZ = E // PLANE
    S = E * cap
    ROWS = D // LANE
    NP = WG.shape[0]
    PC = D // NP
    FF = WG.shape[2]
    CH = PLANE * cap
    dp = lax.axis_index("dp")
    me = lax.axis_index("expert")
    core, xlo = lax.rem(dp, 2), lax.div(dp, 2)
    sib_dp = 2 * xlo + (1 - core)
    crs_dp = 2 * (1 - xlo) + core
    sibling, across = (sib_dp, me), (crs_dp, me)
    my_z, my_y, my_x = lax.div(me, PLANE), lax.rem(lax.div(me, 2), NY), lax.rem(me, 2)

    def partner(dz, i):
        dy, dx = lax.div(i, 2), lax.rem(i, 2)
        e = lax.rem(my_z + dz, NZ) * PLANE + lax.rem(my_y + dy, NY) * 2 + lax.rem(my_x + dx, 2)
        return lax.rem(dp + 2 * dx, 4), e

    barrier = pltpu.get_barrier_semaphore()

    def greet(k, carry):
        pl.semaphore_signal(barrier, inc=1, device_id=partner(lax.div(k, PLANE), lax.rem(k, PLANE)), device_id_type=MESH)
        return carry

    lax.fori_loop(1, E, greet, 0)
    pl.semaphore_signal(barrier, inc=1, device_id=sibling, device_id_type=MESH)
    pl.semaphore_signal(barrier, inc=1, device_id=across, device_id_type=MESH)

    ins = []
    for i, (src, dst) in enumerate(((routes_in, routes), (probs_in, probs_t), (tok_in, tok), (cot_in, cot))):
        ins.append(pltpu.make_async_copy(src, dst, in_sem.at[i]))
        ins[-1].start()

    eye = lax.broadcasted_iota(jnp.int32, (T, T), 0) == lax.broadcasted_iota(jnp.int32, (T, T), 1)

    def column(row):
        return jnp.sum(jnp.where(eye, row, jnp.zeros_like(row)), axis=1, keepdims=True)

    ins[0].wait()
    r0, r1 = column(routes[0:1, :]), column(routes[1:2, :])
    iota_e = lax.broadcasted_iota(jnp.int32, (T, E), 1)
    h0, h1 = r0 == iota_e, r1 == iota_e
    hits = (jnp.where(h0, 1.0, 0.0) + jnp.where(h1, 1.0, 0.0)).astype(BF16)
    tri = jnp.where(
        lax.broadcasted_iota(jnp.int32, (T, T), 0) > lax.broadcasted_iota(jnp.int32, (T, T), 1), 1.0, 0.0
    ).astype(BF16)
    before = mm(tri, hits)
    for k, (r, h) in enumerate(((r0, h0), (r1, h1))):
        rank = jnp.sum(jnp.where(h, before, 0.0), axis=1, keepdims=True).astype(jnp.int32)
        slot_s[:, k : k + 1] = jnp.where(rank < cap, r * cap + rank, S)

    def send_block(a, src, dst, dz, i):
        d, e = partner(dz, i)
        pltpu.make_async_remote_copy(
            src.at[pl.ds(e * cap, cap)],
            dst.at[pl.ds(me * cap, cap)],
            a2a_send.at[a],
            a2a_recv.at[a],
            device_id=(d, e),
            device_id_type=MESH,
        ).start()

    def exchange(a, fill, src, dst, filled=False):
        def send_plane(dz):
            def one(i, c):
                send_block(a, src, dst, dz, i)
                return c

            lax.fori_loop(0, PLANE, one, 0)

        def plane(q, carry):
            half = lax.div(q + 1, 2)
            dz = lax.rem(NZ // 2 + half * (2 * lax.rem(q, 2) - 1), NZ)
            fill(lax.rem(my_z + dz, NZ) * CH)
            send_plane(dz)
            return carry

        if filled:
            send_plane(NZ // 2)
        lax.fori_loop(1 if filled else 0, NZ - 1, plane, 0)
        fill(my_z * CH)
        mine = pl.ds(me * cap, cap)
        pltpu.make_async_copy(src.at[mine], dst.at[mine], a2a_loc.at[a]).start()

        def rest(i, c):
            send_block(a, src, dst, 0, i)
            return c

        lax.fori_loop(1, PLANE, rest, 0)

    def arrived(a, src, dst):
        block = dst.at[pl.ds(0, S - cap)]
        pltpu.make_async_copy(block, block, a2a_recv.at[a]).wait()
        mine = pl.ds(me * cap, cap)
        pltpu.make_async_copy(src.at[mine], dst.at[mine], a2a_loc.at[a]).wait()

    def sent(a, src):
        block = src.at[pl.ds(0, S - cap)]
        pltpu.make_async_copy(block, block, a2a_send.at[a]).wait()

    def lay_rows(v, dst, base):
        for j in range(ROWS):
            scr[pl.ds(j, CH, stride=ROWS), :] = v[:, j * LANE : (j + 1) * LANE]
        dst[pl.ds(base, CH)] = scr[pl.ds(0, CH * ROWS), :].reshape(CH, ROWS, LANE).astype(BF16)

    def onehot(k, base, n):
        return jnp.where(
            slot_s[:, k : k + 1] == lax.broadcasted_iota(jnp.int32, (T, n), 1) + base, 1.0, 0.0
        )

    def fill_x(base):
        pick = (onehot(0, base, CH) + onehot(1, base, CH)).astype(BF16)
        lay_rows(mm_first(pick, tok[...]), xs, base)

    def fill_g(base):
        v = mm_first(onehot(0, base, CH).astype(BF16), rg[0:T, :])
        v += mm_first(onehot(1, base, CH).astype(BF16), rg[T : 2 * T, :])
        lay_rows(v, gs, base)

    first = lax.rem(my_z + NZ // 2, NZ) * CH
    ins[2].wait()
    fill_x(first)
    pl.semaphore_wait(barrier, E + 1)
    mats = ((wg_in, WG), (wu_in, WU), (wd_in, WD))
    ag = []
    for m, (src, full) in enumerate(mats):
        c = pltpu.make_async_remote_copy(
            src, full.at[dp], ag_send.at[m], ag_cross.at[m], device_id=across, device_id_type=MESH
        )
        c.start()
        s = pltpu.make_async_remote_copy(
            src, full.at[dp], ag_send.at[3 + m], ag_sib.at[m], device_id=sibling, device_id_type=MESH
        )
        s.start()
        l = pltpu.make_async_copy(src, full.at[dp], ag_loc.at[m])
        l.start()
        ag.append((c, s, l))

    exchange(0, fill_x, xs, xr, True)
    ins[1].wait()
    ins[3].wait()
    for k in range(2):
        probs[:, k : k + 1] = column(probs_t[k : k + 1, :])
        rg[k * T : (k + 1) * T, :] = (probs[:, k : k + 1] * cot[...].astype(F32)).astype(BF16)
    exchange(1, fill_g, gs, gr)

    def forward_weights(m):
        full = mats[m][1]
        ag[m][0].wait_recv()
        f = pltpu.make_async_remote_copy(
            full.at[crs_dp], full.at[crs_dp], ag_fwd_s.at[m], ag_fwd_r.at[m], device_id=sibling, device_id_type=MESH
        )
        f.start()
        return f

    def weights_here(m, f):
        ag[m][2].wait()
        ag[m][1].wait_recv()
        f.wait_recv()

    def unpack(src):
        step = 16 * cap

        def chunk(c, carry):
            rows = pl.ds(pl.multiple_of(c * step, 16), step)
            scr[pl.ds(0, step * ROWS), :] = src[rows].astype(F32).reshape(step * ROWS, LANE)
            for j in range(ROWS):
                p, o = divmod(j * LANE, PC)
                X[p, rows, o : o + LANE] = scr[pl.ds(j, step, stride=ROWS), :].astype(BF16)
            return carry

        lax.fori_loop(0, S // step, chunk, 0)

    fwd = [forward_weights(0), forward_weights(1)]
    arrived(0, xs, xr)
    unpack(xr)
    weights_here(0, fwd[0])
    weights_here(1, fwd[1])

    def up_tile(n, carry):
        cols = pl.ds(pl.multiple_of(n * TILE, TILE), TILE)
        gate = mm(X[0], WG[0, :, cols])
        up = mm(X[0], WU[0, :, cols])
        for p in range(1, NP):
            gate += mm(X[p], WG[p, :, cols])
            up += mm(X[p], WU[p, :, cols])
        s = jax.nn.sigmoid(gate)
        act = gate * s
        A[:, cols] = up * (s * (1.0 + gate * (1.0 - s)))
        B[:, cols] = act
        HID[:, cols] = (act * up).astype(BF16)
        return carry

    lax.fori_loop(0, FF // TILE, up_tile, 0)
    fwd.append(forward_weights(2))
    weights_here(2, fwd[2])

    def rows_out(p, v):
        for j in range(PC // LANE):
            scr[pl.ds(p * (PC // LANE) + j, S, stride=ROWS), :] = v[:, j * LANE : (j + 1) * LANE]

    def fill_from_scr(dst):
        def fill(base):
            dst[pl.ds(base, CH)] = (
                scr[pl.ds(pl.multiple_of(base * ROWS, ROWS), CH * ROWS), :].reshape(CH, ROWS, LANE).astype(BF16)
            )

        return fill

    for p in range(NP):
        rows_out(p, mm(HID[...], WD[p]))
    exchange(2, fill_from_scr(os_), os_, orr)

    for p in range(NP):
        XT[p] = X[p].T
    HT[...] = HID[...].T

    arrived(1, gs, gr)
    unpack(gr)

    def to_sibling(k, buf_s, buf_r, s):
        c = pltpu.make_async_remote_copy(
            buf_s, buf_r, sib_ss.at[k, s], sib_rs.at[k, s], device_id=sibling, device_id_type=MESH
        )
        c.start()
        return c

    def to_across(k, buf_s, buf_r):
        c = pltpu.make_async_remote_copy(
            buf_s, buf_r, crs_ss.at[k], crs_rs.at[k], device_id=across, device_id_type=MESH
        )
        c.start()
        return c

    def part_down(p):
        return mm(HT[...], X[p])

    def part_gu(m, p):
        return mm(XT[p], (DG, DU)[m][...])

    sib = {}
    for s in range(2):
        sibd_s[s] = part_down(2 * s + (1 - core)).astype(BF16)
        sib[2, s] = to_sibling(2, sibd_s.at[s], sibd_r.at[s], s)

    def dh_tile(n, carry):
        cols = pl.ds(pl.multiple_of(n * TILE, TILE), TILE)
        dh = mm_last(X[0], WD[0, cols, :])
        for p in range(1, NP):
            dh += mm_last(X[p], WD[p, cols, :])
        DG[:, cols] = (dh * A[:, cols]).astype(BF16)
        DU[:, cols] = (dh * B[:, cols]).astype(BF16)
        return carry

    lax.fori_loop(0, FF // TILE, dh_tile, 0)
    for m in range(2):
        for s in range(2):
            sib_s[m, s] = part_gu(m, 2 * s + (1 - core)).astype(BF16)
            sib[m, s] = to_sibling(m, sib_s.at[m, s], sib_r.at[m, s], s)

    for s in range(2):
        sib[2, s].wait_recv()
    crsd_s[...] = (part_down(crs_dp) + sibd_r[1 - xlo].astype(F32)).astype(BF16)
    crs = [None, None, to_across(2, crsd_s, crsd_r)]
    for m in range(2):
        for s in range(2):
            sib[m, s].wait_recv()
        crs_s[m] = (part_gu(m, crs_dp) + sib_r[m, 1 - xlo].astype(F32)).astype(BF16)
        crs[m] = to_across(m, crs_s.at[m], crs_r.at[m])

    sent(0, xs)
    for p in range(NP):
        rows_out(p, mm_last(DG[...], WG[p]) + mm_last(DU[...], WU[p]))
    exchange(3, fill_from_scr(xs), xs, dxr)

    find[...] = part_down(dp) + sibd_r[xlo].astype(F32)
    for m in range(2):
        fin[m] = part_gu(m, dp) + sib_r[m, xlo].astype(F32)

    arrived(2, os_, orr)
    unpack(orr)
    p0, p1 = onehot(0, 0, S).astype(BF16), onehot(1, 0, S).astype(BF16)
    dg0 = jnp.zeros((T, 1), F32)
    dg1 = jnp.zeros((T, 1), F32)
    for p in range(NP):
        cols = slice(p * PC, (p + 1) * PC)
        k0, k1 = mm(p0, X[p]), mm(p1, X[p])
        lay[:, cols] = (probs[:, 0:1] * k0 + probs[:, 1:2] * k1).astype(BF16)
        c32 = cot[:, cols].astype(F32)
        dg0 += jnp.sum(c32 * k0, axis=1, keepdims=True)
        dg1 += jnp.sum(c32 * k1, axis=1, keepdims=True)
    for k, v in enumerate((dg0, dg1)):
        dgate[k : k + 1, :] = jnp.sum(jnp.where(eye, v, 0.0), axis=0, keepdims=True)

    outs = []
    for i, (src, dst) in enumerate(((lay, lay_o), (dgate, dgate_o), (slot_s, slot_o))):
        outs.append(pltpu.make_async_copy(src, dst, out_sem.at[3 + i]))
        outs[-1].start()
    crs[2].wait_recv()
    find[...] += crsd_r[...].astype(F32)
    outs.append(pltpu.make_async_copy(find, gd_o, out_sem.at[2]))
    outs[-1].start()
    for m, o in enumerate((gg_o, gu_o)):
        crs[m].wait_recv()
        fin[m] += crs_r[m].astype(F32)
        outs.append(pltpu.make_async_copy(fin.at[m], o, out_sem.at[m]))
        outs[-1].start()

    arrived(3, xs, dxr)

    sent(1, gs)
    sent(2, os_)
    sent(3, xs)
    for m in range(3):
        ag[m][0].wait_send()
        ag[m][1].wait_send()
        fwd[m].wait_send()
        crs[m].wait_send()
        for s in range(2):
            sib[m, s].wait_send()
    for o in outs:
        o.wait()


def finish(
    cap,
    slots, dxr, lay, dgate, gg, gu, gd,
    dtok_o, lay_o, dgate_o, gg_o, gu_o, gd_o,
    got, dtok, scr, Y, gg_v, gu_v, gd_v, lay_v, dgate_v, got_sem, in_sem, out_sem, dtok_sem,
):
    T, D = dtok.shape
    S, ROWS, _ = got.shape
    NP, _, PC = Y.shape
    step = 16 * cap
    loads = []
    for c in range(S // step):
        rows = pl.ds(c * step, step)
        loads.append(pltpu.make_async_copy(dxr.at[rows], got.at[rows], got_sem.at[c]))
        loads[-1].start()
    through = ((gg, gg_v, gg_o), (gu, gu_v, gu_o), (gd, gd_v, gd_o), (lay, lay_v, lay_o), (dgate, dgate_v, dgate_o))
    copies = []
    for i, (src, held, dst) in enumerate(through):
        copies.append(pltpu.make_async_copy(src, held, in_sem.at[i]))
        copies[-1].start()
    stores = []
    for c in range(S // step):
        loads[c].wait()
        rows = pl.ds(c * step, step)
        scr[...] = got[rows].astype(F32).reshape(step * ROWS, LANE)
        for j in range(ROWS):
            p, o = divmod(j * LANE, PC)
            Y[p, rows, o : o + LANE] = scr[pl.ds(j, step, stride=ROWS), :].astype(BF16)
        while len(stores) < min(2 * c, len(through)):
            i = len(stores)
            copies[i].wait()
            stores.append(pltpu.make_async_copy(*through[i][1:], out_sem.at[i]))
            stores[-1].start()
    iota = lax.broadcasted_iota(jnp.int32, (T, S), 1)
    both = jnp.where((slots[:, 0:1] == iota) | (slots[:, 1:2] == iota), 1.0, 0.0).astype(BF16)
    for p in range(NP):
        dtok[:, p * PC : (p + 1) * PC] = mm(both, Y[p]).astype(BF16)
    out = pltpu.make_async_copy(dtok, dtok_o, dtok_sem)
    out.start()
    for c in stores:
        c.wait()
    out.wait()


def on_device(tokens, routes, gate_probs, cotangent, w_gate, w_up, w_down):
    T, D = tokens.shape
    E = lax.axis_size("expert")
    NP = lax.axis_size("dp")
    PC, FF = w_gate.shape[1:]
    cap = max(2, 3 * T * routes.shape[1] // (2 * E))
    S = E * cap
    ROWS = D // LANE
    rows_buf = pltpu.VMEM((S, ROWS, LANE), BF16)
    dma = pltpu.SemaphoreType.DMA
    vmem = pl.BlockSpec(memory_space=pltpu.VMEM)
    hbm = pl.BlockSpec(memory_space=pl.ANY)
    scratch = [
        pltpu.VMEM((T, D), BF16),
        pltpu.VMEM((2, T), jnp.int32),
        pltpu.VMEM((2, T), F32),
        pltpu.VMEM((T, D), BF16),
        pltpu.VMEM((T, 2), F32),
        pltpu.VMEM((T, D), BF16),
        pltpu.VMEM((2, T), F32),
        pltpu.VMEM((T, 2), jnp.int32),
        pltpu.VMEM((2 * T, D), BF16),
        *([rows_buf] * 6),
        pltpu.VMEM((NP, S, PC), BF16),
        pltpu.VMEM((NP, PC, S), BF16),
        pltpu.VMEM((FF, S), BF16),
        pltpu.VMEM((NP, PC, FF), BF16),
        pltpu.VMEM((NP, PC, FF), BF16),
        pltpu.VMEM((NP, FF, PC), BF16),
        pltpu.VMEM((S, FF), F32),
        pltpu.VMEM((S, FF), F32),
        *([pltpu.VMEM((S, FF), BF16)] * 3),
        pltpu.VMEM((S * ROWS, LANE), F32),
        pltpu.VMEM((2, 2, PC, FF), BF16),
        pltpu.VMEM((2, 2, PC, FF), BF16),
        pltpu.VMEM((2, FF, PC), BF16),
        pltpu.VMEM((2, FF, PC), BF16),
        pltpu.VMEM((2, PC, FF), BF16),
        pltpu.VMEM((2, PC, FF), BF16),
        pltpu.VMEM((FF, PC), BF16),
        pltpu.VMEM((FF, PC), BF16),
        pltpu.VMEM((2, PC, FF), F32),
        pltpu.VMEM((FF, PC), F32),
        dma((4,)), dma((4,)), dma((4,)),
        dma((3,)), dma((6,)), dma((3,)), dma((3,)), dma((3,)), dma((3,)),
        dma((3, 2)), dma((3, 2)), dma((3,)), dma((3,)), dma((4,)), dma((6,)),
    ]
    lay_shape = jax.ShapeDtypeStruct((T, D), BF16)
    dgate_shape = jax.ShapeDtypeStruct((2, T), F32)
    grads = (
        jax.ShapeDtypeStruct((PC, FF), F32),
        jax.ShapeDtypeStruct((PC, FF), F32),
        jax.ShapeDtypeStruct((FF, PC), F32),
    )
    lay, dgate, slots, dxr, gg, gu, gd = pl.pallas_call(
        functools.partial(kernel, cap),
        out_shape=(
            lay_shape,
            dgate_shape,
            jax.ShapeDtypeStruct((T, 2), jnp.int32),
            jax.ShapeDtypeStruct((S, ROWS, LANE), BF16),
            *grads,
        ),
        in_specs=[hbm] * 7,
        out_specs=(hbm,) * 7,
        scratch_shapes=scratch,
        compiler_params=pltpu.CompilerParams(
            collective_id=0, has_side_effects=True, vmem_limit_bytes=64000 * 1024
        ),
    )(tokens, routes.T, gate_probs.T, cotangent, w_gate[0], w_up[0], w_down[0])
    dtok, lay, dgate, gg, gu, gd = pl.pallas_call(
        functools.partial(finish, cap),
        out_shape=(lay_shape, lay_shape, dgate_shape, *grads),
        in_specs=[vmem] + [hbm] * 6,
        out_specs=(hbm,) * 6,
        scratch_shapes=[
            pltpu.VMEM((S, ROWS, LANE), BF16),
            pltpu.VMEM((T, D), BF16),
            pltpu.VMEM((16 * cap * ROWS, LANE), F32),
            pltpu.VMEM((NP, S, PC), BF16),
            pltpu.VMEM((PC, FF), F32),
            pltpu.VMEM((PC, FF), F32),
            pltpu.VMEM((FF, PC), F32),
            pltpu.VMEM((T, D), BF16),
            pltpu.VMEM((2, T), F32),
            dma((S // (16 * cap),)),
            dma((5,)),
            dma((5,)),
            dma,
        ],
        compiler_params=pltpu.CompilerParams(vmem_limit_bytes=64000 * 1024),
    )(slots, dxr, lay, dgate, gg, gu, gd)
    return lay, dtok, dgate.T, gg[None], gu[None], gd[None]


def solution(mesh):
    rows = P(("dp", "expert"), None)
    weights = (P("expert", "dp", None), P("expert", "dp", None), P("expert", None, "dp"))
    return jax.shard_map(
        on_device,
        mesh=mesh,
        in_specs=(rows, rows, rows, rows, *weights),
        out_specs=(rows, rows, rows, *weights),
        check_vma=False,
    )
```

```python
import functools

import jax
import jax.numpy as jnp
from jax import lax
from jax.experimental import pallas as pl
from jax.experimental.pallas import tpu as pltpu
from jax.sharding import PartitionSpec as P

MESH = pl.DeviceIdType.MESH
LANE = 128
PLANE = 8
NY = 4
TILE = 256
F32 = jnp.float32
BF16 = jnp.bfloat16


def mm(a, b):
    return jnp.dot(a, b, preferred_element_type=F32)


def mm_last(a, b):
    return lax.dot_general(a, b, (((1,), (1,)), ((), ())), preferred_element_type=F32)


def mm_first(a, b):
    return lax.dot_general(a, b, (((0,), (0,)), ((), ())), preferred_element_type=F32)


def kernel(
    cap,
    tok_in, routes_in, probs_in, cot_in, wg_in, wu_in, wd_in,
    lay_o, dgate_o, slot_o, dxr, gg_o, gu_o, gd_o,
    toks, rts, prb, cots, lay, dgate, slot_s, rg, xs, gs, os_, xr, gr, orr, X, XT, HT, WG, WU, WD, A, B, HID, DG, DU, scr,
    sib_s, sib_r, sibd_s, sibd_r, crs_s, crs_r, crsd_s, crsd_r, fin, find,
    a2a_send, a2a_recv, a2a_loc, ag_loc, ag_send, ag_cross, ag_sib, ag_fwd_s, ag_fwd_r,
    sib_ss, sib_rs, crs_ss, crs_rs, in_sem, out_sem, near_s, near_r,
):
    _, T, D = toks.shape
    E = lax.axis_size("expert")
    NZ = E // PLANE
    S = E * cap
    ROWS = D // LANE
    NP = WG.shape[0]
    PC = D // NP
    FF = WG.shape[2]
    CH = PLANE * cap
    dp = lax.axis_index("dp")
    me = lax.axis_index("expert")
    core, xlo = lax.rem(dp, 2), lax.div(dp, 2)
    sib_dp = 2 * xlo + (1 - core)
    crs_dp = 2 * (1 - xlo) + core
    sibling, across = (sib_dp, me), (crs_dp, me)
    my_z, my_y, my_x = lax.div(me, PLANE), lax.rem(lax.div(me, 2), NY), lax.rem(me, 2)

    def partner(dz, i):
        dy, dx = lax.div(i, 2), lax.rem(i, 2)
        e = lax.rem(my_z + dz, NZ) * PLANE + lax.rem(my_y + dy, NY) * 2 + lax.rem(my_x + dx, 2)
        return lax.rem(dp + 2 * dx, 4), e

    barrier = pltpu.get_barrier_semaphore()

    def greet(k, carry):
        pl.semaphore_signal(barrier, inc=1, device_id=partner(lax.div(k, PLANE), lax.rem(k, PLANE)), device_id_type=MESH)
        return carry

    lax.fori_loop(1, E, greet, 0, unroll=7)
    pl.semaphore_signal(barrier, inc=1, device_id=sibling, device_id_type=MESH)
    pl.semaphore_signal(barrier, inc=1, device_id=across, device_id_type=MESH)

    ins = []
    for i, (src, dst) in enumerate(((routes_in, rts), (probs_in, prb), (tok_in, toks), (cot_in, cots))):
        ins.append(pltpu.make_async_copy(src, dst.at[0], in_sem.at[i]))
        ins[-1].start()

    eye = lax.broadcasted_iota(jnp.int32, (T, T), 0) == lax.broadcasted_iota(jnp.int32, (T, T), 1)

    def column(row):
        return jnp.sum(jnp.where(eye, row, jnp.zeros_like(row)), axis=1, keepdims=True)

    iota_e = lax.broadcasted_iota(jnp.int32, (T, E), 1)
    tri = jnp.where(
        lax.broadcasted_iota(jnp.int32, (T, T), 0) > lax.broadcasted_iota(jnp.int32, (T, T), 1), 1.0, 0.0
    ).astype(BF16)

    def find_slots(s):
        r0, r1 = column(rts[s, 0:1, :]), column(rts[s, 1:2, :])
        h0, h1 = r0 == iota_e, r1 == iota_e
        hits = (jnp.where(h0, 1.0, 0.0) + jnp.where(h1, 1.0, 0.0)).astype(BF16)
        before = mm(tri, hits)
        for k, (r, h) in enumerate(((r0, h0), (r1, h1))):
            rank = jnp.sum(jnp.where(h, before, 0.0), axis=1, keepdims=True).astype(jnp.int32)
            slot_s[s, :, k : k + 1] = jnp.where(rank < cap, r * cap + rank, S)

    def find_route_grads(s):
        for k in range(2):
            rg[k * T : (k + 1) * T, :] = (column(prb[s, k : k + 1, :]) * cots[s].astype(F32)).astype(BF16)

    def send_block(a, src, row, dst, owner, dz, i):
        d, e = partner(dz, i)
        pltpu.make_async_remote_copy(
            src.at[pl.ds(row + lax.rem(e, PLANE) * cap, cap)],
            dst.at[pl.ds(owner * cap, cap)],
            a2a_send.at[a],
            a2a_recv.at[a],
            device_id=(d, e),
            device_id_type=MESH,
        ).start()

    def keep_block(a, src, row, dst, owner):
        pltpu.make_async_copy(
            src.at[pl.ds(row + lax.rem(me, PLANE) * cap, cap)], dst.at[pl.ds(owner * cap, cap)], a2a_loc.at[a]
        ).start()

    def own_plane(a, src, row, dst):
        keep_block(a, src, row, dst, me)

        def one(i, c):
            send_block(a, src, row, dst, me, 0, i)
            return c

        lax.fori_loop(1, PLANE, one, 0)

    def exchange(a, fill, src, dst):
        def plane(q, carry):
            half = lax.div(q + 1, 2)
            dz = lax.rem(NZ // 2 + half * (2 * lax.rem(q, 2) - 1), NZ)
            row = lax.rem(my_z + dz, NZ) * CH
            fill(row)

            def one(i, c):
                send_block(a, src, row, dst, me, dz, i)
                return c

            lax.fori_loop(0, PLANE, one, 0)
            return carry

        lax.fori_loop(0, NZ - 1, plane, 0)
        fill(my_z * CH)
        own_plane(a, src, my_z * CH, dst)

    def relay(a, prepare, fill, src, dst):
        def side(d, carry):
            prepare(d)
            way = 1 - 2 * d
            owner = lax.rem(my_z + NZ - way, NZ) * PLANE + lax.rem(me, PLANE)

            def plane(t, c0):
                q = NZ // 2 - 1 - t
                dz = lax.rem(NZ + way * q, NZ)
                row = (1 + (NZ // 2) * d + q) * CH
                fill(1 + d, lax.rem(my_z + dz, NZ) * CH, row)

                def one(i, c1):
                    other_half = (q == NZ // 2 - 1) & (lax.rem(my_x + i, 2) != d)
                    stays = (q == 0) & (i == 0)

                    @pl.when(stays)
                    def _():
                        keep_block(a, src, row, dst, owner)

                    @pl.when(jnp.logical_not(stays | other_half))
                    def _():
                        send_block(a, src, row, dst, owner, dz, i)

                    return c1

                lax.fori_loop(0, PLANE, one, 0)
                return c0

            lax.fori_loop(0, NZ // 2, plane, 0)
            return carry

        lax.fori_loop(0, 2, side, 0)

    def arrived(a, dst, kept):
        block = dst.at[pl.ds(0, S - kept * cap)]
        pltpu.make_async_copy(block, block, a2a_recv.at[a]).wait()
        block = dst.at[pl.ds(0, kept * cap)]
        pltpu.make_async_copy(block, block, a2a_loc.at[a]).wait()

    def sent(a, src, kept):
        block = src.at[pl.ds(0, S - kept * cap)]
        pltpu.make_async_copy(block, block, a2a_send.at[a]).wait()

    def lay_rows(v, dst, base):
        for j in range(ROWS):
            scr[pl.ds(j, CH, stride=ROWS), :] = v[:, j * LANE : (j + 1) * LANE]
        dst[pl.ds(base, CH)] = scr[pl.ds(0, CH * ROWS), :].reshape(CH, ROWS, LANE).astype(BF16)

    def onehot(k, base, n, s=0):
        return jnp.where(
            slot_s[s, :, k : k + 1] == lax.broadcasted_iota(jnp.int32, (T, n), 1) + base, 1.0, 0.0
        )

    def fill_x(s, base, row):
        pick = (onehot(0, base, CH, s) + onehot(1, base, CH, s)).astype(BF16)
        lay_rows(mm_first(pick, toks[s]), xs, row)

    def fill_g(s, base, row):
        v = mm_first(onehot(0, base, CH, s).astype(BF16), rg[0:T, :])
        v += mm_first(onehot(1, base, CH, s).astype(BF16), rg[T : 2 * T, :])
        lay_rows(v, gs, row)

    def to_neighbours(kind, src, buf):
        copies = []
        for d in range(2):
            c = pltpu.make_async_remote_copy(
                src,
                buf.at[1 + d],
                near_s.at[kind, d],
                near_r.at[kind, d],
                device_id=partner((1, NZ - 1)[d], 0),
                device_id_type=MESH,
            )
            c.start()
            copies.append(c)
        return copies

    def from_neighbour(kind, buf, d):
        pltpu.make_async_copy(buf.at[1 + d], buf.at[1 + d], near_r.at[kind, d]).wait()

    pl.semaphore_wait(barrier, E + 1)
    near = to_neighbours(0, routes_in, rts) + to_neighbours(2, tok_in, toks) + to_neighbours(1, probs_in, prb)

    mats = ((wg_in, WG), (wu_in, WU), (wd_in, WD))
    ag = []
    for m, (src, full) in enumerate(mats):
        c = pltpu.make_async_remote_copy(
            src, full.at[dp], ag_send.at[m], ag_cross.at[m], device_id=across, device_id_type=MESH
        )
        c.start()
        s = pltpu.make_async_remote_copy(
            src, full.at[dp], ag_send.at[3 + m], ag_sib.at[m], device_id=sibling, device_id_type=MESH
        )
        s.start()
        l = pltpu.make_async_copy(src, full.at[dp], ag_loc.at[m])
        l.start()
        ag.append((c, s, l))

    near += to_neighbours(3, cot_in, cots)
    ins[0].wait()
    find_slots(0)
    ins[2].wait()
    fill_x(0, my_z * CH, 0)
    own_plane(0, xs, 0, xr)
    ins[1].wait()
    ins[3].wait()
    find_route_grads(0)
    fill_g(0, my_z * CH, 0)
    own_plane(1, gs, 0, gr)

    def prepare_x(d):
        from_neighbour(0, rts, d)
        find_slots(1 + d)
        from_neighbour(2, toks, d)

    def prepare_g(d):
        from_neighbour(1, prb, d)
        from_neighbour(3, cots, d)
        find_route_grads(1 + d)

    relay(0, prepare_x, fill_x, xs, xr)
    relay(1, prepare_g, fill_g, gs, gr)

    def forward_weights(m):
        full = mats[m][1]
        ag[m][0].wait_recv()
        f = pltpu.make_async_remote_copy(
            full.at[crs_dp], full.at[crs_dp], ag_fwd_s.at[m], ag_fwd_r.at[m], device_id=sibling, device_id_type=MESH
        )
        f.start()
        return f

    def weights_here(m, f):
        ag[m][2].wait()
        ag[m][1].wait_recv()
        f.wait_recv()

    def unpack(src):
        step = 16 * cap

        def chunk(c, carry):
            rows = pl.ds(pl.multiple_of(c * step, 16), step)
            scr[pl.ds(0, step * ROWS), :] = src[rows].astype(F32).reshape(step * ROWS, LANE)
            for j in range(ROWS):
                p, o = divmod(j * LANE, PC)
                X[p, rows, o : o + LANE] = scr[pl.ds(j, step, stride=ROWS), :].astype(BF16)
            return carry

        lax.fori_loop(0, S // step, chunk, 0)

    fwd = [forward_weights(0), forward_weights(1)]
    arrived(0, xr, 3)
    unpack(xr)
    weights_here(0, fwd[0])
    weights_here(1, fwd[1])

    def up_tile(n, carry):
        cols = pl.ds(pl.multiple_of(n * TILE, TILE), TILE)
        gate = mm(X[0], WG[0, :, cols])
        up = mm(X[0], WU[0, :, cols])
        for p in range(1, NP):
            gate += mm(X[p], WG[p, :, cols])
            up += mm(X[p], WU[p, :, cols])
        s = jax.nn.sigmoid(gate)
        act = gate * s
        A[:, cols] = up * (s * (1.0 + gate * (1.0 - s)))
        B[:, cols] = act
        HID[:, cols] = (act * up).astype(BF16)
        return carry

    lax.fori_loop(0, FF // TILE, up_tile, 0)
    fwd.append(forward_weights(2))
    weights_here(2, fwd[2])

    def rows_out(p, v):
        for j in range(PC // LANE):
            scr[pl.ds(p * (PC // LANE) + j, S, stride=ROWS), :] = v[:, j * LANE : (j + 1) * LANE]

    def fill_from_scr(dst):
        def fill(base):
            dst[pl.ds(base, CH)] = (
                scr[pl.ds(pl.multiple_of(base * ROWS, ROWS), CH * ROWS), :].reshape(CH, ROWS, LANE).astype(BF16)
            )

        return fill

    for p in range(NP):
        rows_out(p, mm(HID[...], WD[p]))
    exchange(2, fill_from_scr(os_), os_, orr)

    for p in range(NP):
        XT[p] = X[p].T
    HT[...] = HID[...].T

    arrived(1, gr, 3)
    unpack(gr)

    def to_sibling(k, buf_s, buf_r, s):
        c = pltpu.make_async_remote_copy(
            buf_s, buf_r, sib_ss.at[k, s], sib_rs.at[k, s], device_id=sibling, device_id_type=MESH
        )
        c.start()
        return c

    def to_across(k, buf_s, buf_r):
        c = pltpu.make_async_remote_copy(
            buf_s, buf_r, crs_ss.at[k], crs_rs.at[k], device_id=across, device_id_type=MESH
        )
        c.start()
        return c

    def part_down(p):
        return mm(HT[...], X[p])

    def part_gu(m, p):
        return mm(XT[p], (DG, DU)[m][...])

    sib = {}
    for s in range(2):
        sibd_s[s] = part_down(2 * s + (1 - core)).astype(BF16)
        sib[2, s] = to_sibling(2, sibd_s.at[s], sibd_r.at[s], s)

    def dh_tile(n, carry):
        cols = pl.ds(pl.multiple_of(n * TILE, TILE), TILE)
        dh = mm_last(X[0], WD[0, cols, :])
        for p in range(1, NP):
            dh += mm_last(X[p], WD[p, cols, :])
        DG[:, cols] = (dh * A[:, cols]).astype(BF16)
        DU[:, cols] = (dh * B[:, cols]).astype(BF16)
        return carry

    lax.fori_loop(0, FF // TILE, dh_tile, 0)
    for m in range(2):
        for s in range(2):
            sib_s[m, s] = part_gu(m, 2 * s + (1 - core)).astype(BF16)
            sib[m, s] = to_sibling(m, sib_s.at[m, s], sib_r.at[m, s], s)

    for s in range(2):
        sib[2, s].wait_recv()
    crsd_s[...] = (part_down(crs_dp) + sibd_r[1 - xlo].astype(F32)).astype(BF16)
    crs = [None, None, to_across(2, crsd_s, crsd_r)]
    for m in range(2):
        for s in range(2):
            sib[m, s].wait_recv()
        crs_s[m] = (part_gu(m, crs_dp) + sib_r[m, 1 - xlo].astype(F32)).astype(BF16)
        crs[m] = to_across(m, crs_s.at[m], crs_r.at[m])

    sent(0, xs, 3)
    for p in range(NP):
        rows_out(p, mm_last(DG[...], WG[p]) + mm_last(DU[...], WU[p]))
    exchange(3, fill_from_scr(xs), xs, dxr)

    find[...] = part_down(dp) + sibd_r[xlo].astype(F32)
    for m in range(2):
        fin[m] = part_gu(m, dp) + sib_r[m, xlo].astype(F32)

    arrived(2, orr, 1)
    unpack(orr)
    p0, p1 = onehot(0, 0, S).astype(BF16), onehot(1, 0, S).astype(BF16)
    w0, w1 = column(prb[0, 0:1, :]), column(prb[0, 1:2, :])
    dg0 = jnp.zeros((T, 1), F32)
    dg1 = jnp.zeros((T, 1), F32)
    for p in range(NP):
        cols = slice(p * PC, (p + 1) * PC)
        k0, k1 = mm(p0, X[p]), mm(p1, X[p])
        lay[:, cols] = (w0 * k0 + w1 * k1).astype(BF16)
        c32 = cots[0, :, cols].astype(F32)
        dg0 += jnp.sum(c32 * k0, axis=1, keepdims=True)
        dg1 += jnp.sum(c32 * k1, axis=1, keepdims=True)
    for k, v in enumerate((dg0, dg1)):
        dgate[k : k + 1, :] = jnp.sum(jnp.where(eye, v, 0.0), axis=0, keepdims=True)

    outs = []
    for i, (src, dst) in enumerate(((lay, lay_o), (dgate, dgate_o), (slot_s.at[0], slot_o))):
        outs.append(pltpu.make_async_copy(src, dst, out_sem.at[3 + i]))
        outs[-1].start()
    crs[2].wait_recv()
    find[...] += crsd_r[...].astype(F32)
    outs.append(pltpu.make_async_copy(find, gd_o, out_sem.at[2]))
    outs[-1].start()
    for m, o in enumerate((gg_o, gu_o)):
        crs[m].wait_recv()
        fin[m] += crs_r[m].astype(F32)
        outs.append(pltpu.make_async_copy(fin.at[m], o, out_sem.at[m]))
        outs[-1].start()

    arrived(3, dxr, 1)

    sent(1, gs, 3)
    sent(2, os_, 1)
    sent(3, xs, 1)
    for c in near:
        c.wait_send()
    for m in range(3):
        ag[m][0].wait_send()
        ag[m][1].wait_send()
        fwd[m].wait_send()
        crs[m].wait_send()
        for s in range(2):
            sib[m, s].wait_send()
    for o in outs:
        o.wait()


def finish(
    cap,
    slots, dxr, lay, dgate, gg, gu, gd,
    dtok_o, lay_o, dgate_o, gg_o, gu_o, gd_o,
    got, dtok, scr, Y, gg_v, gu_v, gd_v, lay_v, dgate_v, got_sem, in_sem, out_sem, dtok_sem,
):
    T, D = dtok.shape
    S, ROWS, _ = got.shape
    NP, _, PC = Y.shape
    step = 16 * cap
    loads = []
    for c in range(S // step):
        rows = pl.ds(c * step, step)
        loads.append(pltpu.make_async_copy(dxr.at[rows], got.at[rows], got_sem.at[c]))
        loads[-1].start()
    through = ((gg, gg_v, gg_o), (gu, gu_v, gu_o), (gd, gd_v, gd_o), (lay, lay_v, lay_o), (dgate, dgate_v, dgate_o))
    copies = []
    for i, (src, held, dst) in enumerate(through):
        copies.append(pltpu.make_async_copy(src, held, in_sem.at[i]))
        copies[-1].start()
    stores = []
    for c in range(S // step):
        loads[c].wait()
        rows = pl.ds(c * step, step)
        scr[...] = got[rows].astype(F32).reshape(step * ROWS, LANE)
        for j in range(ROWS):
            p, o = divmod(j * LANE, PC)
            Y[p, rows, o : o + LANE] = scr[pl.ds(j, step, stride=ROWS), :].astype(BF16)
        while len(stores) < min(2 * c, len(through)):
            i = len(stores)
            copies[i].wait()
            stores.append(pltpu.make_async_copy(*through[i][1:], out_sem.at[i]))
            stores[-1].start()
    iota = lax.broadcasted_iota(jnp.int32, (T, S), 1)
    both = jnp.where((slots[:, 0:1] == iota) | (slots[:, 1:2] == iota), 1.0, 0.0).astype(BF16)
    for p in range(NP):
        dtok[:, p * PC : (p + 1) * PC] = mm(both, Y[p]).astype(BF16)
    out = pltpu.make_async_copy(dtok, dtok_o, dtok_sem)
    out.start()
    for c in stores:
        c.wait()
    out.wait()


def on_device(tokens, routes, gate_probs, cotangent, w_gate, w_up, w_down):
    T, D = tokens.shape
    E = lax.axis_size("expert")
    NP = lax.axis_size("dp")
    PC, FF = w_gate.shape[1:]
    cap = max(2, 3 * T * routes.shape[1] // (2 * E))
    S = E * cap
    ROWS = D // LANE
    rows_buf = pltpu.VMEM((S, ROWS, LANE), BF16)
    relay_buf = pltpu.VMEM((S + PLANE * cap, ROWS, LANE), BF16)
    dma = pltpu.SemaphoreType.DMA
    vmem = pl.BlockSpec(memory_space=pltpu.VMEM)
    hbm = pl.BlockSpec(memory_space=pl.ANY)
    scratch = [
        pltpu.VMEM((3, T, D), BF16),
        pltpu.VMEM((3, 2, T), jnp.int32),
        pltpu.VMEM((3, 2, T), F32),
        pltpu.VMEM((3, T, D), BF16),
        pltpu.VMEM((T, D), BF16),
        pltpu.VMEM((2, T), F32),
        pltpu.VMEM((3, T, 2), jnp.int32),
        pltpu.VMEM((2 * T, D), BF16),
        *([relay_buf] * 2),
        *([rows_buf] * 4),
        pltpu.VMEM((NP, S, PC), BF16),
        pltpu.VMEM((NP, PC, S), BF16),
        pltpu.VMEM((FF, S), BF16),
        pltpu.VMEM((NP, PC, FF), BF16),
        pltpu.VMEM((NP, PC, FF), BF16),
        pltpu.VMEM((NP, FF, PC), BF16),
        pltpu.VMEM((S, FF), F32),
        pltpu.VMEM((S, FF), F32),
        *([pltpu.VMEM((S, FF), BF16)] * 3),
        pltpu.VMEM((S * ROWS, LANE), F32),
        pltpu.VMEM((2, 2, PC, FF), BF16),
        pltpu.VMEM((2, 2, PC, FF), BF16),
        pltpu.VMEM((2, FF, PC), BF16),
        pltpu.VMEM((2, FF, PC), BF16),
        pltpu.VMEM((2, PC, FF), BF16),
        pltpu.VMEM((2, PC, FF), BF16),
        pltpu.VMEM((FF, PC), BF16),
        pltpu.VMEM((FF, PC), BF16),
        pltpu.VMEM((2, PC, FF), F32),
        pltpu.VMEM((FF, PC), F32),
        dma((4,)), dma((4,)), dma((4,)),
        dma((3,)), dma((6,)), dma((3,)), dma((3,)), dma((3,)), dma((3,)),
        dma((3, 2)), dma((3, 2)), dma((3,)), dma((3,)), dma((4,)), dma((6,)), dma((4, 2)), dma((4, 2)),
    ]
    lay_shape = jax.ShapeDtypeStruct((T, D), BF16)
    dgate_shape = jax.ShapeDtypeStruct((2, T), F32)
    grads = (
        jax.ShapeDtypeStruct((PC, FF), F32),
        jax.ShapeDtypeStruct((PC, FF), F32),
        jax.ShapeDtypeStruct((FF, PC), F32),
    )
    lay, dgate, slots, dxr, gg, gu, gd = pl.pallas_call(
        functools.partial(kernel, cap),
        out_shape=(
            lay_shape,
            dgate_shape,
            jax.ShapeDtypeStruct((T, 2), jnp.int32),
            jax.ShapeDtypeStruct((S, ROWS, LANE), BF16),
            *grads,
        ),
        in_specs=[hbm] * 7,
        out_specs=(hbm,) * 7,
        scratch_shapes=scratch,
        compiler_params=pltpu.CompilerParams(
            collective_id=0, has_side_effects=True, vmem_limit_bytes=64000 * 1024
        ),
    )(tokens, routes.T, gate_probs.T, cotangent, w_gate[0], w_up[0], w_down[0])
    dtok, lay, dgate, gg, gu, gd = pl.pallas_call(
        functools.partial(finish, cap),
        out_shape=(lay_shape, lay_shape, dgate_shape, *grads),
        in_specs=[vmem] + [hbm] * 6,
        out_specs=(hbm,) * 6,
        scratch_shapes=[
            pltpu.VMEM((S, ROWS, LANE), BF16),
            pltpu.VMEM((T, D), BF16),
            pltpu.VMEM((16 * cap * ROWS, LANE), F32),
            pltpu.VMEM((NP, S, PC), BF16),
            pltpu.VMEM((PC, FF), F32),
            pltpu.VMEM((PC, FF), F32),
            pltpu.VMEM((FF, PC), F32),
            pltpu.VMEM((T, D), BF16),
            pltpu.VMEM((2, T), F32),
            dma((S // (16 * cap),)),
            dma((5,)),
            dma((5,)),
            dma,
        ],
        compiler_params=pltpu.CompilerParams(vmem_limit_bytes=64000 * 1024),
    )(slots, dxr, lay, dgate, gg, gu, gd)
    return lay, dtok, dgate.T, gg[None], gu[None], gd[None]


def solution(mesh):
    rows = P(("dp", "expert"), None)
    weights = (P("expert", "dp", None), P("expert", "dp", None), P("expert", None, "dp"))
    return jax.shard_map(
        on_device,
        mesh=mesh,
        in_specs=(rows, rows, rows, rows, *weights),
        out_specs=(rows, rows, rows, *weights),
        check_vma=False,
    )
```

```python
import functools

import jax
import jax.numpy as jnp
from jax import lax
from jax.experimental import pallas as pl
from jax.experimental.pallas import tpu as pltpu
from jax.sharding import PartitionSpec as P

MESH = pl.DeviceIdType.MESH
LANE = 128
PLANE = 8
NY = 4
TILE = 256
F32 = jnp.float32
BF16 = jnp.bfloat16


def mm(a, b):
    return jnp.dot(a, b, preferred_element_type=F32)


def mm_last(a, b):
    return lax.dot_general(a, b, (((1,), (1,)), ((), ())), preferred_element_type=F32)


def mm_first(a, b):
    return lax.dot_general(a, b, (((0,), (0,)), ((), ())), preferred_element_type=F32)


def kernel(
    cap,
    tok_in, routes_in, probs_in, cot_in, wg_in, wu_in, wd_in,
    lay_o, dgate_o, slot_o, dxr, gg_o, gu_o, gd_o,
    toks, rts, prb, cots, lay, dgate, slot_s, rg, xs, gs, os_, xr, gr, orr, X, XT, HT, WG, WU, WD, A, B, HID, DG, DU, scr,
    sib_s, sib_r, sibd_s, sibd_r, crs_s, crs_r, crsd_s, crsd_r, fin, find,
    a2a_send, a2a_recv, a2a_loc, ag_loc, ag_send, ag_cross, ag_sib, ag_fwd_s, ag_fwd_r,
    sib_ss, sib_rs, crs_ss, crs_rs, in_sem, out_sem, near_s, near_r,
):
    _, T, D = toks.shape
    E = lax.axis_size("expert")
    NZ = E // PLANE
    S = E * cap
    ROWS = D // LANE
    NP = WG.shape[0]
    PC = D // NP
    FF = WG.shape[2]
    CH = PLANE * cap
    dp = lax.axis_index("dp")
    me = lax.axis_index("expert")
    core, xlo = lax.rem(dp, 2), lax.div(dp, 2)
    sib_dp = 2 * xlo + (1 - core)
    crs_dp = 2 * (1 - xlo) + core
    sibling, across = (sib_dp, me), (crs_dp, me)
    my_z, my_y, my_x = lax.div(me, PLANE), lax.rem(lax.div(me, 2), NY), lax.rem(me, 2)

    def partner(dz, i):
        dy, dx = lax.div(i, 2), lax.rem(i, 2)
        e = lax.rem(my_z + dz, NZ) * PLANE + lax.rem(my_y + dy, NY) * 2 + lax.rem(my_x + dx, 2)
        return lax.rem(dp + 2 * dx, 4), e

    barrier = pltpu.get_barrier_semaphore()

    def greet(k, carry):
        pl.semaphore_signal(barrier, inc=1, device_id=partner(lax.div(k, PLANE), lax.rem(k, PLANE)), device_id_type=MESH)
        return carry

    lax.fori_loop(1, E, greet, 0, unroll=7)
    pl.semaphore_signal(barrier, inc=1, device_id=sibling, device_id_type=MESH)
    pl.semaphore_signal(barrier, inc=1, device_id=across, device_id_type=MESH)

    ins = []
    for i, (src, dst) in enumerate(((routes_in, rts), (probs_in, prb), (tok_in, toks), (cot_in, cots))):
        ins.append(pltpu.make_async_copy(src, dst.at[0], in_sem.at[i]))
        ins[-1].start()

    eye = lax.broadcasted_iota(jnp.int32, (T, T), 0) == lax.broadcasted_iota(jnp.int32, (T, T), 1)

    def column(row):
        return jnp.sum(jnp.where(eye, row, jnp.zeros_like(row)), axis=1, keepdims=True)

    iota_e = lax.broadcasted_iota(jnp.int32, (T, E), 1)
    tri = jnp.where(
        lax.broadcasted_iota(jnp.int32, (T, T), 0) > lax.broadcasted_iota(jnp.int32, (T, T), 1), 1.0, 0.0
    ).astype(BF16)

    def find_slots(s):
        r0, r1 = column(rts[s, 0:1, :]), column(rts[s, 1:2, :])
        h0, h1 = r0 == iota_e, r1 == iota_e
        hits = (jnp.where(h0, 1.0, 0.0) + jnp.where(h1, 1.0, 0.0)).astype(BF16)
        before = mm(tri, hits)
        for k, (r, h) in enumerate(((r0, h0), (r1, h1))):
            rank = jnp.sum(jnp.where(h, before, 0.0), axis=1, keepdims=True).astype(jnp.int32)
            slot_s[s, :, k : k + 1] = jnp.where(rank < cap, r * cap + rank, S)

    def find_route_grads(s):
        for k in range(2):
            rg[k * T : (k + 1) * T, :] = (column(prb[s, k : k + 1, :]) * cots[s].astype(F32)).astype(BF16)

    def send_block(a, src, row, dst, owner, dz, i):
        d, e = partner(dz, i)
        pltpu.make_async_remote_copy(
            src.at[pl.ds(row + lax.rem(e, PLANE) * cap, cap)],
            dst.at[pl.ds(owner * cap, cap)],
            a2a_send.at[a],
            a2a_recv.at[a],
            device_id=(d, e),
            device_id_type=MESH,
        ).start()

    def keep_block(a, src, row, dst, owner):
        pltpu.make_async_copy(
            src.at[pl.ds(row + lax.rem(me, PLANE) * cap, cap)], dst.at[pl.ds(owner * cap, cap)], a2a_loc.at[a]
        ).start()

    def own_plane(a, src, row, dst):
        keep_block(a, src, row, dst, me)

        def one(i, c):
            send_block(a, src, row, dst, me, 0, i)
            return c

        lax.fori_loop(1, PLANE, one, 0)

    def exchange(a, fill, src, dst):
        def plane(q, carry):
            half = lax.div(q + 1, 2)
            dz = lax.rem(NZ // 2 + half * (2 * lax.rem(q, 2) - 1), NZ)
            row = lax.rem(my_z + dz, NZ) * CH
            fill(row)

            def one(i, c):
                send_block(a, src, row, dst, me, dz, i)
                return c

            lax.fori_loop(0, PLANE, one, 0)
            return carry

        lax.fori_loop(0, NZ - 1, plane, 0)
        fill(my_z * CH)
        own_plane(a, src, my_z * CH, dst)

    def relay(a, prepare, fill, src, dst):
        def side(d, carry):
            prepare(d)
            way = 1 - 2 * d
            owner = lax.rem(my_z + NZ - way, NZ) * PLANE + lax.rem(me, PLANE)

            def plane(t, c0):
                q = NZ // 2 - 1 - t
                dz = lax.rem(NZ + way * q, NZ)
                row = (1 + (NZ // 2) * d + q) * CH
                fill(1 + d, lax.rem(my_z + dz, NZ) * CH, row)

                def one(i, c1):
                    other_half = (q == NZ // 2 - 1) & (lax.rem(my_x + i, 2) != d)
                    stays = (q == 0) & (i == 0)

                    @pl.when(stays)
                    def _():
                        keep_block(a, src, row, dst, owner)

                    @pl.when(jnp.logical_not(stays | other_half))
                    def _():
                        send_block(a, src, row, dst, owner, dz, i)

                    return c1

                lax.fori_loop(0, PLANE, one, 0)
                return c0

            lax.fori_loop(0, NZ // 2, plane, 0)
            return carry

        lax.fori_loop(0, 2, side, 0)

    def arrived(a, dst, kept):
        block = dst.at[pl.ds(0, S - kept * cap)]
        pltpu.make_async_copy(block, block, a2a_recv.at[a]).wait()
        block = dst.at[pl.ds(0, kept * cap)]
        pltpu.make_async_copy(block, block, a2a_loc.at[a]).wait()

    def sent(a, src, kept):
        block = src.at[pl.ds(0, S - kept * cap)]
        pltpu.make_async_copy(block, block, a2a_send.at[a]).wait()

    def lay_rows(v, dst, base):
        for j in range(ROWS):
            scr[pl.ds(j, CH, stride=ROWS), :] = v[:, j * LANE : (j + 1) * LANE]
        dst[pl.ds(base, CH)] = scr[pl.ds(0, CH * ROWS), :].reshape(CH, ROWS, LANE).astype(BF16)

    def onehot(k, base, n, s=0):
        return jnp.where(
            slot_s[s, :, k : k + 1] == lax.broadcasted_iota(jnp.int32, (T, n), 1) + base, 1.0, 0.0
        )

    def fill_x(s, base, row):
        pick = (onehot(0, base, CH, s) + onehot(1, base, CH, s)).astype(BF16)
        lay_rows(mm_first(pick, toks[s]), xs, row)

    def fill_g(s, base, row):
        v = mm_first(onehot(0, base, CH, s).astype(BF16), rg[0:T, :])
        v += mm_first(onehot(1, base, CH, s).astype(BF16), rg[T : 2 * T, :])
        lay_rows(v, gs, row)

    def to_neighbours(kind, src, buf):
        copies = []
        for d in range(2):
            c = pltpu.make_async_remote_copy(
                src,
                buf.at[1 + d],
                near_s.at[kind, d],
                near_r.at[kind, d],
                device_id=partner((1, NZ - 1)[d], 0),
                device_id_type=MESH,
            )
            c.start()
            copies.append(c)
        return copies

    def from_neighbour(kind, buf, d):
        pltpu.make_async_copy(buf.at[1 + d], buf.at[1 + d], near_r.at[kind, d]).wait()

    pl.semaphore_wait(barrier, E + 1)
    near = to_neighbours(0, routes_in, rts) + to_neighbours(2, tok_in, toks) + to_neighbours(1, probs_in, prb)

    mats = ((wg_in, WG), (wu_in, WU), (wd_in, WD))
    ag = []
    for m, (src, full) in enumerate(mats):
        c = pltpu.make_async_remote_copy(
            src, full.at[dp], ag_send.at[m], ag_cross.at[m], device_id=across, device_id_type=MESH
        )
        c.start()
        s = pltpu.make_async_remote_copy(
            src, full.at[dp], ag_send.at[3 + m], ag_sib.at[m], device_id=sibling, device_id_type=MESH
        )
        s.start()
        l = pltpu.make_async_copy(src, full.at[dp], ag_loc.at[m])
        l.start()
        ag.append((c, s, l))

    near += to_neighbours(3, cot_in, cots)
    ins[0].wait()
    find_slots(0)
    ins[2].wait()
    fill_x(0, my_z * CH, 0)
    own_plane(0, xs, 0, xr)
    ins[1].wait()
    ins[3].wait()
    find_route_grads(0)
    fill_g(0, my_z * CH, 0)
    own_plane(1, gs, 0, gr)

    def prepare_x(d):
        from_neighbour(0, rts, d)
        find_slots(1 + d)
        from_neighbour(2, toks, d)

    def prepare_g(d):
        from_neighbour(1, prb, d)
        from_neighbour(3, cots, d)
        find_route_grads(1 + d)

    relay(0, prepare_x, fill_x, xs, xr)
    relay(1, prepare_g, fill_g, gs, gr)

    def forward_weights(m):
        full = mats[m][1]
        ag[m][0].wait_recv()
        f = pltpu.make_async_remote_copy(
            full.at[crs_dp], full.at[crs_dp], ag_fwd_s.at[m], ag_fwd_r.at[m], device_id=sibling, device_id_type=MESH
        )
        f.start()
        return f

    def weights_here(m, f):
        ag[m][2].wait()
        ag[m][1].wait_recv()
        f.wait_recv()

    def unpack(src):
        step = 16 * cap

        def chunk(c, carry):
            rows = pl.ds(pl.multiple_of(c * step, 16), step)
            scr[pl.ds(0, step * ROWS), :] = src[rows].astype(F32).reshape(step * ROWS, LANE)
            for j in range(ROWS):
                p, o = divmod(j * LANE, PC)
                X[p, rows, o : o + LANE] = scr[pl.ds(j, step, stride=ROWS), :].astype(BF16)
            return carry

        lax.fori_loop(0, S // step, chunk, 0)

    fwd = [forward_weights(0), forward_weights(1)]
    arrived(0, xr, 3)
    unpack(xr)
    weights_here(0, fwd[0])
    weights_here(1, fwd[1])

    def up_tile(n, carry):
        cols = pl.ds(pl.multiple_of(n * TILE, TILE), TILE)
        gate = mm(X[0], WG[0, :, cols])
        up = mm(X[0], WU[0, :, cols])
        for p in range(1, NP):
            gate += mm(X[p], WG[p, :, cols])
            up += mm(X[p], WU[p, :, cols])
        s = jax.nn.sigmoid(gate)
        act = gate * s
        A[:, cols] = up * (s * (1.0 + gate * (1.0 - s)))
        B[:, cols] = act
        HID[:, cols] = (act * up).astype(BF16)
        return carry

    lax.fori_loop(0, FF // TILE, up_tile, 0)
    fwd.append(forward_weights(2))
    weights_here(2, fwd[2])

    def rows_out(p, v):
        for j in range(PC // LANE):
            scr[pl.ds(p * (PC // LANE) + j, S, stride=ROWS), :] = v[:, j * LANE : (j + 1) * LANE]

    def fill_from_scr(dst):
        def fill(base):
            dst[pl.ds(base, CH)] = (
                scr[pl.ds(pl.multiple_of(base * ROWS, ROWS), CH * ROWS), :].reshape(CH, ROWS, LANE).astype(BF16)
            )

        return fill

    for p in range(NP):
        rows_out(p, mm(HID[...], WD[p]))
    exchange(2, fill_from_scr(os_), os_, orr)

    for p in range(NP):
        XT[p] = X[p].T
    HT[...] = HID[...].T

    arrived(1, gr, 3)
    unpack(gr)

    def to_sibling(k, buf_s, buf_r, s):
        c = pltpu.make_async_remote_copy(
            buf_s, buf_r, sib_ss.at[k, s], sib_rs.at[k, s], device_id=sibling, device_id_type=MESH
        )
        c.start()
        return c

    def to_across(k, buf_s, buf_r):
        c = pltpu.make_async_remote_copy(
            buf_s, buf_r, crs_ss.at[k], crs_rs.at[k], device_id=across, device_id_type=MESH
        )
        c.start()
        return c

    def part_down(p):
        return mm(HT[...], X[p])

    def part_gu(m, p):
        return mm(XT[p], (DG, DU)[m][...])

    sib = {}
    for s in range(2):
        sibd_s[s] = part_down(2 * s + (1 - core)).astype(BF16)
        sib[2, s] = to_sibling(2, sibd_s.at[s], sibd_r.at[s], s)

    def dh_tile(n, carry):
        cols = pl.ds(pl.multiple_of(n * TILE, TILE), TILE)
        dh = mm_last(X[0], WD[0, cols, :])
        for p in range(1, NP):
            dh += mm_last(X[p], WD[p, cols, :])
        DG[:, cols] = (dh * A[:, cols]).astype(BF16)
        DU[:, cols] = (dh * B[:, cols]).astype(BF16)
        return carry

    lax.fori_loop(0, FF // TILE, dh_tile, 0)
    for m in range(2):
        for s in range(2):
            sib_s[m, s] = part_gu(m, 2 * s + (1 - core)).astype(BF16)
            sib[m, s] = to_sibling(m, sib_s.at[m, s], sib_r.at[m, s], s)

    for s in range(2):
        sib[2, s].wait_recv()
    crsd_s[...] = (part_down(crs_dp) + sibd_r[1 - xlo].astype(F32)).astype(BF16)
    crs = [None, None, to_across(2, crsd_s, crsd_r)]
    for m in range(2):
        for s in range(2):
            sib[m, s].wait_recv()
        crs_s[m] = (part_gu(m, crs_dp) + sib_r[m, 1 - xlo].astype(F32)).astype(BF16)
        crs[m] = to_across(m, crs_s.at[m], crs_r.at[m])

    sent(0, xs, 3)
    for p in range(NP):
        rows_out(p, mm_last(DG[...], WG[p]) + mm_last(DU[...], WU[p]))
    exchange(3, fill_from_scr(xs), xs, dxr)

    find[...] = part_down(dp) + sibd_r[xlo].astype(F32)
    for m in range(2):
        fin[m] = part_gu(m, dp) + sib_r[m, xlo].astype(F32)

    arrived(2, orr, 1)
    unpack(orr)
    p0, p1 = onehot(0, 0, S).astype(BF16), onehot(1, 0, S).astype(BF16)
    w0, w1 = column(prb[0, 0:1, :]), column(prb[0, 1:2, :])
    dg0 = jnp.zeros((T, 1), F32)
    dg1 = jnp.zeros((T, 1), F32)
    for p in range(NP):
        cols = slice(p * PC, (p + 1) * PC)
        k0, k1 = mm(p0, X[p]), mm(p1, X[p])
        lay[:, cols] = (w0 * k0 + w1 * k1).astype(BF16)
        c32 = cots[0, :, cols].astype(F32)
        dg0 += jnp.sum(c32 * k0, axis=1, keepdims=True)
        dg1 += jnp.sum(c32 * k1, axis=1, keepdims=True)
    for k, v in enumerate((dg0, dg1)):
        dgate[k : k + 1, :] = jnp.sum(jnp.where(eye, v, 0.0), axis=0, keepdims=True)

    outs = []
    for i, (src, dst) in enumerate(((lay, lay_o), (dgate, dgate_o), (slot_s.at[0], slot_o))):
        outs.append(pltpu.make_async_copy(src, dst, out_sem.at[3 + i]))
        outs[-1].start()
    crs[2].wait_recv()
    find[...] += crsd_r[...].astype(F32)
    outs.append(pltpu.make_async_copy(find, gd_o, out_sem.at[2]))
    outs[-1].start()
    for m, o in enumerate((gg_o, gu_o)):
        crs[m].wait_recv()
        fin[m] += crs_r[m].astype(F32)
        outs.append(pltpu.make_async_copy(fin.at[m], o, out_sem.at[m]))
        outs[-1].start()

    arrived(3, dxr, 1)

    sent(1, gs, 3)
    sent(2, os_, 1)
    sent(3, xs, 1)
    for c in near:
        c.wait_send()
    for m in range(3):
        ag[m][0].wait_send()
        ag[m][1].wait_send()
        fwd[m].wait_send()
        crs[m].wait_send()
        for s in range(2):
            sib[m, s].wait_send()
    for o in outs:
        o.wait()


def finish(
    cap,
    slots_in, dxr, lay, dgate, gg, gu, gd,
    dtok_o, lay_o, dgate_o, gg_o, gu_o, gd_o,
    got, dtok, scr, Y, gg_v, gu_v, gd_v, lay_v, dgate_v, slots, got_sem, in_sem, out_sem, dtok_sem, slot_sem,
):
    T, D = dtok.shape
    S, ROWS, _ = got.shape
    NP, _, PC = Y.shape
    step = 16 * cap
    loads = []
    for c in range(S // step):
        rows = pl.ds(c * step, step)
        loads.append(pltpu.make_async_copy(dxr.at[rows], got.at[rows], got_sem.at[c]))
        loads[-1].start()
    slot_load = pltpu.make_async_copy(slots_in, slots, slot_sem)
    slot_load.start()
    through = ((gg, gg_v, gg_o), (gu, gu_v, gu_o), (gd, gd_v, gd_o), (lay, lay_v, lay_o), (dgate, dgate_v, dgate_o))
    copies = []
    for i, (src, held, dst) in enumerate(through):
        copies.append(pltpu.make_async_copy(src, held, in_sem.at[i]))
        copies[-1].start()
    stores = []
    for c in range(S // step):
        loads[c].wait()
        rows = pl.ds(c * step, step)
        scr[pl.ds(0, step * ROWS), :] = got[rows].astype(F32).reshape(step * ROWS, LANE)
        for j in range(ROWS):
            p, o = divmod(j * LANE, PC)
            Y[p, rows, o : o + LANE] = scr[pl.ds(j, step, stride=ROWS), :].astype(BF16)
        while len(stores) < min(2 * c, len(through)):
            i = len(stores)
            copies[i].wait()
            stores.append(pltpu.make_async_copy(*through[i][1:], out_sem.at[i]))
            stores[-1].start()
    slot_load.wait()
    iota = lax.broadcasted_iota(jnp.int32, (T, S), 1)
    both = jnp.where((slots[:, 0:1] == iota) | (slots[:, 1:2] == iota), 1.0, 0.0).astype(BF16)
    for p in range(NP):
        dtok[:, p * PC : (p + 1) * PC] = mm(both, Y[p]).astype(BF16)
    out = pltpu.make_async_copy(dtok, dtok_o, dtok_sem)
    out.start()
    for c in stores:
        c.wait()
    out.wait()


def on_device(tokens, routes, gate_probs, cotangent, w_gate, w_up, w_down):
    T, D = tokens.shape
    E = lax.axis_size("expert")
    NP = lax.axis_size("dp")
    PC, FF = w_gate.shape[1:]
    cap = max(2, 3 * T * routes.shape[1] // (2 * E))
    S = E * cap
    ROWS = D // LANE
    rows_buf = pltpu.VMEM((S, ROWS, LANE), BF16)
    relay_buf = pltpu.VMEM((S + PLANE * cap, ROWS, LANE), BF16)
    dma = pltpu.SemaphoreType.DMA
    hbm = pl.BlockSpec(memory_space=pl.ANY)
    scratch = [
        pltpu.VMEM((3, T, D), BF16),
        pltpu.VMEM((3, 2, T), jnp.int32),
        pltpu.VMEM((3, 2, T), F32),
        pltpu.VMEM((3, T, D), BF16),
        pltpu.VMEM((T, D), BF16),
        pltpu.VMEM((2, T), F32),
        pltpu.VMEM((3, T, 2), jnp.int32),
        pltpu.VMEM((2 * T, D), BF16),
        *([relay_buf] * 2),
        *([rows_buf] * 4),
        pltpu.VMEM((NP, S, PC), BF16),
        pltpu.VMEM((NP, PC, S), BF16),
        pltpu.VMEM((FF, S), BF16),
        pltpu.VMEM((NP, PC, FF), BF16),
        pltpu.VMEM((NP, PC, FF), BF16),
        pltpu.VMEM((NP, FF, PC), BF16),
        pltpu.VMEM((S, FF), F32),
        pltpu.VMEM((S, FF), F32),
        *([pltpu.VMEM((S, FF), BF16)] * 3),
        pltpu.VMEM((S * ROWS + 8 * ROWS, LANE), F32),
        pltpu.VMEM((2, 2, PC, FF), BF16),
        pltpu.VMEM((2, 2, PC, FF), BF16),
        pltpu.VMEM((2, FF, PC), BF16),
        pltpu.VMEM((2, FF, PC), BF16),
        pltpu.VMEM((2, PC, FF), BF16),
        pltpu.VMEM((2, PC, FF), BF16),
        pltpu.VMEM((FF, PC), BF16),
        pltpu.VMEM((FF, PC), BF16),
        pltpu.VMEM((2, PC, FF), F32),
        pltpu.VMEM((FF, PC), F32),
        dma((4,)), dma((4,)), dma((4,)),
        dma((3,)), dma((6,)), dma((3,)), dma((3,)), dma((3,)), dma((3,)),
        dma((3, 2)), dma((3, 2)), dma((3,)), dma((3,)), dma((4,)), dma((6,)), dma((4, 2)), dma((4, 2)),
    ]
    lay_shape = jax.ShapeDtypeStruct((T, D), BF16)
    dgate_shape = jax.ShapeDtypeStruct((2, T), F32)
    grads = (
        jax.ShapeDtypeStruct((PC, FF), F32),
        jax.ShapeDtypeStruct((PC, FF), F32),
        jax.ShapeDtypeStruct((FF, PC), F32),
    )
    lay, dgate, slots, dxr, gg, gu, gd = pl.pallas_call(
        functools.partial(kernel, cap),
        out_shape=(
            lay_shape,
            dgate_shape,
            jax.ShapeDtypeStruct((T, 2), jnp.int32),
            jax.ShapeDtypeStruct((S, ROWS, LANE), BF16),
            *grads,
        ),
        in_specs=[hbm] * 7,
        out_specs=(hbm,) * 7,
        scratch_shapes=scratch,
        compiler_params=pltpu.CompilerParams(
            collective_id=0, has_side_effects=True, vmem_limit_bytes=64000 * 1024
        ),
    )(tokens, routes.T, gate_probs.T, cotangent, w_gate[0], w_up[0], w_down[0])
    dtok, lay, dgate, gg, gu, gd = pl.pallas_call(
        functools.partial(finish, cap),
        out_shape=(lay_shape, lay_shape, dgate_shape, *grads),
        in_specs=[hbm] * 7,
        out_specs=(hbm,) * 6,
        scratch_shapes=[
            pltpu.VMEM((S, ROWS, LANE), BF16),
            pltpu.VMEM((T, D), BF16),
            pltpu.VMEM((16 * cap * ROWS + 8 * ROWS, LANE), F32),
            pltpu.VMEM((NP, S, PC), BF16),
            pltpu.VMEM((PC, FF), F32),
            pltpu.VMEM((PC, FF), F32),
            pltpu.VMEM((FF, PC), F32),
            pltpu.VMEM((T, D), BF16),
            pltpu.VMEM((2, T), F32),
            pltpu.VMEM((T, 2), jnp.int32),
            dma((S // (16 * cap),)),
            dma((5,)),
            dma((5,)),
            dma,
            dma,
        ],
        compiler_params=pltpu.CompilerParams(vmem_limit_bytes=64000 * 1024),
    )(slots, dxr, lay, dgate, gg, gu, gd)
    return lay, dtok, dgate.T, gg[None], gu[None], gd[None]


def solution(mesh):
    rows = P(("dp", "expert"), None)
    weights = (P("expert", "dp", None), P("expert", "dp", None), P("expert", None, "dp"))
    return jax.shard_map(
        on_device,
        mesh=mesh,
        in_specs=(rows, rows, rows, rows, *weights),
        out_specs=(rows, rows, rows, *weights),
        check_vma=False,
    )
```

```python
import functools

import jax
import jax.numpy as jnp
from jax import lax
from jax.experimental import pallas as pl
from jax.experimental.pallas import tpu as pltpu
from jax.sharding import PartitionSpec as P

MESH = pl.DeviceIdType.MESH
LANE = 128
PLANE = 8
NY = 4
TILE = 256
F32 = jnp.float32
BF16 = jnp.bfloat16


def mm(a, b):
    return jnp.dot(a, b, preferred_element_type=F32)


def mm_last(a, b):
    return lax.dot_general(a, b, (((1,), (1,)), ((), ())), preferred_element_type=F32)


def mm_first(a, b):
    return lax.dot_general(a, b, (((0,), (0,)), ((), ())), preferred_element_type=F32)


def kernel(
    cap,
    tok_in, routes_in, probs_in, cot_in, wg_in, wu_in, wd_in,
    lay_o, dgate_o, slot_o, dxr, gg_o, gu_o, gd_o,
    toks, rts, prb, cots, lay, dgate, slot_s, rg, xs, gs, os_, xr, gr, orr, X, XT, HT, WG, WU, WD, A, B, HID, DG, DU, scr,
    sib_s, sib_r, sibd_s, sibd_r, crs_s, crs_r, crsd_s, crsd_r, fin, find,
    a2a_send, a2a_recv, a2a_loc, ag_loc, ag_send, ag_cross, ag_sib, ag_fwd_s, ag_fwd_r,
    sib_ss, sib_rs, crs_ss, crs_rs, in_sem, out_sem, near_s, near_r,
):
    _, T, D = toks.shape
    E = lax.axis_size("expert")
    NZ = E // PLANE
    S = E * cap
    ROWS = D // LANE
    NP = WG.shape[0]
    PC = D // NP
    FF = WG.shape[2]
    CH = PLANE * cap
    dp = lax.axis_index("dp")
    me = lax.axis_index("expert")
    core, xlo = lax.rem(dp, 2), lax.div(dp, 2)
    sib_dp = 2 * xlo + (1 - core)
    crs_dp = 2 * (1 - xlo) + core
    sibling, across = (sib_dp, me), (crs_dp, me)
    my_z, my_y, my_x = lax.div(me, PLANE), lax.rem(lax.div(me, 2), NY), lax.rem(me, 2)

    def partner(dz, i):
        dy, dx = lax.div(i, 2), lax.rem(i, 2)
        e = lax.rem(my_z + dz, NZ) * PLANE + lax.rem(my_y + dy, NY) * 2 + lax.rem(my_x + dx, 2)
        return lax.rem(dp + 2 * dx, 4), e

    barrier = pltpu.get_barrier_semaphore()

    def greet(k, carry):
        pl.semaphore_signal(barrier, inc=1, device_id=partner(lax.div(k, PLANE), lax.rem(k, PLANE)), device_id_type=MESH)
        return carry

    lax.fori_loop(1, E, greet, 0, unroll=7)
    pl.semaphore_signal(barrier, inc=1, device_id=sibling, device_id_type=MESH)
    pl.semaphore_signal(barrier, inc=1, device_id=across, device_id_type=MESH)

    ins = []
    for i, (src, dst) in enumerate(((routes_in, rts), (probs_in, prb), (tok_in, toks), (cot_in, cots))):
        ins.append(pltpu.make_async_copy(src, dst.at[0], in_sem.at[i]))
        ins[-1].start()

    eye = lax.broadcasted_iota(jnp.int32, (T, T), 0) == lax.broadcasted_iota(jnp.int32, (T, T), 1)

    def column(row):
        return jnp.sum(jnp.where(eye, row, jnp.zeros_like(row)), axis=1, keepdims=True)

    iota_e = lax.broadcasted_iota(jnp.int32, (T, E), 1)
    tri = jnp.where(
        lax.broadcasted_iota(jnp.int32, (T, T), 0) > lax.broadcasted_iota(jnp.int32, (T, T), 1), 1.0, 0.0
    ).astype(BF16)

    def find_slots(s):
        r0, r1 = column(rts[s, 0:1, :]), column(rts[s, 1:2, :])
        h0, h1 = r0 == iota_e, r1 == iota_e
        hits = (jnp.where(h0, 1.0, 0.0) + jnp.where(h1, 1.0, 0.0)).astype(BF16)
        before = mm(tri, hits)
        for k, (r, h) in enumerate(((r0, h0), (r1, h1))):
            rank = jnp.sum(jnp.where(h, before, 0.0), axis=1, keepdims=True).astype(jnp.int32)
            slot_s[s, :, k : k + 1] = jnp.where(rank < cap, r * cap + rank, S)

    def find_route_grads(s):
        for k in range(2):
            rg[k * T : (k + 1) * T, :] = (column(prb[s, k : k + 1, :]) * cots[s].astype(F32)).astype(BF16)

    def send_block(a, src, row, dst, owner, dz, i):
        d, e = partner(dz, i)
        pltpu.make_async_remote_copy(
            src.at[pl.ds(row + lax.rem(e, PLANE) * cap, cap)],
            dst.at[pl.ds(owner * cap, cap)],
            a2a_send.at[a],
            a2a_recv.at[a],
            device_id=(d, e),
            device_id_type=MESH,
        ).start()

    def keep_block(a, src, row, dst, owner):
        pltpu.make_async_copy(
            src.at[pl.ds(row + lax.rem(me, PLANE) * cap, cap)], dst.at[pl.ds(owner * cap, cap)], a2a_loc.at[a]
        ).start()

    def own_plane(a, src, row, dst):
        keep_block(a, src, row, dst, me)

        def one(i, c):
            send_block(a, src, row, dst, me, 0, i)
            return c

        lax.fori_loop(1, PLANE, one, 0)

    def exchange(a, fill, src, dst):
        def plane(q, carry):
            half = lax.div(q + 1, 2)
            dz = lax.rem(NZ // 2 + half * (2 * lax.rem(q, 2) - 1), NZ)
            row = lax.rem(my_z + dz, NZ) * CH
            fill(row)

            def one(i, c):
                send_block(a, src, row, dst, me, dz, i)
                return c

            lax.fori_loop(0, PLANE, one, 0)
            return carry

        lax.fori_loop(0, NZ - 1, plane, 0)
        fill(my_z * CH)
        own_plane(a, src, my_z * CH, dst)

    def relay(a, prepare, fill, src, dst):
        def side(d, carry):
            prepare(d)
            way = 1 - 2 * d
            owner = lax.rem(my_z + NZ - way, NZ) * PLANE + lax.rem(me, PLANE)

            def plane(t, c0):
                q = NZ // 2 - 1 - t
                dz = lax.rem(NZ + way * q, NZ)
                row = (1 + (NZ // 2) * d + q) * CH
                fill(1 + d, lax.rem(my_z + dz, NZ) * CH, row)

                def one(i, c1):
                    other_half = (q == NZ // 2 - 1) & (lax.rem(my_x + i, 2) != d)
                    stays = (q == 0) & (i == 0)

                    @pl.when(stays)
                    def _():
                        keep_block(a, src, row, dst, owner)

                    @pl.when(jnp.logical_not(stays | other_half))
                    def _():
                        send_block(a, src, row, dst, owner, dz, i)

                    return c1

                lax.fori_loop(0, PLANE, one, 0)
                return c0

            lax.fori_loop(0, NZ // 2, plane, 0)
            return carry

        lax.fori_loop(0, 2, side, 0)

    def arrived(a, dst, kept):
        block = dst.at[pl.ds(0, S - kept * cap)]
        pltpu.make_async_copy(block, block, a2a_recv.at[a]).wait()
        block = dst.at[pl.ds(0, kept * cap)]
        pltpu.make_async_copy(block, block, a2a_loc.at[a]).wait()

    def sent(a, src, kept):
        block = src.at[pl.ds(0, S - kept * cap)]
        pltpu.make_async_copy(block, block, a2a_send.at[a]).wait()

    def lay_rows(v, dst, base):
        for j in range(ROWS):
            scr[pl.ds(j, CH, stride=ROWS), :] = v[:, j * LANE : (j + 1) * LANE]
        dst[pl.ds(base, CH)] = scr[pl.ds(0, CH * ROWS), :].reshape(CH, ROWS, LANE).astype(BF16)

    def onehot(k, base, n, s=0):
        return jnp.where(
            slot_s[s, :, k : k + 1] == lax.broadcasted_iota(jnp.int32, (T, n), 1) + base, 1.0, 0.0
        )

    def fill_x(s, base, row):
        pick = (onehot(0, base, CH, s) + onehot(1, base, CH, s)).astype(BF16)
        lay_rows(mm_first(pick, toks[s]), xs, row)

    def fill_g(s, base, row):
        v = mm_first(onehot(0, base, CH, s).astype(BF16), rg[0:T, :])
        v += mm_first(onehot(1, base, CH, s).astype(BF16), rg[T : 2 * T, :])
        lay_rows(v, gs, row)

    def to_neighbours(kind, src, buf):
        copies = []
        for d in range(2):
            c = pltpu.make_async_remote_copy(
                src,
                buf.at[1 + d],
                near_s.at[kind, d],
                near_r.at[kind, d],
                device_id=partner((1, NZ - 1)[d], 0),
                device_id_type=MESH,
            )
            c.start()
            copies.append(c)
        return copies

    def from_neighbour(kind, buf, d):
        pltpu.make_async_copy(buf.at[1 + d], buf.at[1 + d], near_r.at[kind, d]).wait()

    pl.semaphore_wait(barrier, E + 1)
    near = to_neighbours(0, routes_in, rts) + to_neighbours(2, tok_in, toks) + to_neighbours(1, probs_in, prb)

    mats = ((wg_in, WG), (wu_in, WU), (wd_in, WD))
    ag = []
    for m, (src, full) in enumerate(mats):
        c = pltpu.make_async_remote_copy(
            src, full.at[dp], ag_send.at[m], ag_cross.at[m], device_id=across, device_id_type=MESH
        )
        c.start()
        s = pltpu.make_async_remote_copy(
            src, full.at[dp], ag_send.at[3 + m], ag_sib.at[m], device_id=sibling, device_id_type=MESH
        )
        s.start()
        l = pltpu.make_async_copy(src, full.at[dp], ag_loc.at[m])
        l.start()
        ag.append((c, s, l))

    near += to_neighbours(3, cot_in, cots)
    ins[0].wait()
    find_slots(0)
    ins[2].wait()
    fill_x(0, my_z * CH, 0)
    own_plane(0, xs, 0, xr)
    ins[1].wait()
    ins[3].wait()
    find_route_grads(0)
    fill_g(0, my_z * CH, 0)
    own_plane(1, gs, 0, gr)

    def prepare_x(d):
        from_neighbour(0, rts, d)
        find_slots(1 + d)
        from_neighbour(2, toks, d)

    def prepare_g(d):
        from_neighbour(1, prb, d)
        from_neighbour(3, cots, d)
        find_route_grads(1 + d)

    relay(0, prepare_x, fill_x, xs, xr)
    relay(1, prepare_g, fill_g, gs, gr)

    def forward_weights(m):
        full = mats[m][1]
        ag[m][0].wait_recv()
        f = pltpu.make_async_remote_copy(
            full.at[crs_dp], full.at[crs_dp], ag_fwd_s.at[m], ag_fwd_r.at[m], device_id=sibling, device_id_type=MESH
        )
        f.start()
        return f

    def weights_here(m, f):
        ag[m][2].wait()
        ag[m][1].wait_recv()
        f.wait_recv()

    def unpack(src):
        step = 16 * cap

        def chunk(c, carry):
            rows = pl.ds(pl.multiple_of(c * step, 16), step)
            scr[pl.ds(0, step * ROWS), :] = src[rows].astype(F32).reshape(step * ROWS, LANE)
            for j in range(ROWS):
                p, o = divmod(j * LANE, PC)
                X[p, rows, o : o + LANE] = scr[pl.ds(j, step, stride=ROWS), :].astype(BF16)
            return carry

        lax.fori_loop(0, S // step, chunk, 0)

    fwd = [forward_weights(0), forward_weights(1)]
    arrived(0, xr, 3)
    unpack(xr)
    weights_here(0, fwd[0])
    weights_here(1, fwd[1])

    def up_tile(n, carry):
        cols = pl.ds(pl.multiple_of(n * TILE, TILE), TILE)
        gate = mm(X[0], WG[0, :, cols])
        up = mm(X[0], WU[0, :, cols])
        for p in range(1, NP):
            gate += mm(X[p], WG[p, :, cols])
            up += mm(X[p], WU[p, :, cols])
        s = jax.nn.sigmoid(gate)
        act = gate * s
        A[:, cols] = up * (s * (1.0 + gate * (1.0 - s)))
        B[:, cols] = act
        HID[:, cols] = (act * up).astype(BF16)
        return carry

    lax.fori_loop(0, FF // TILE, up_tile, 0)
    fwd.append(forward_weights(2))
    weights_here(2, fwd[2])

    def rows_out(p, v):
        for j in range(PC // LANE):
            scr[pl.ds(p * (PC // LANE) + j, S, stride=ROWS), :] = v[:, j * LANE : (j + 1) * LANE]

    def fill_from_scr(dst):
        def fill(base):
            dst[pl.ds(base, CH)] = (
                scr[pl.ds(pl.multiple_of(base * ROWS, ROWS), CH * ROWS), :].reshape(CH, ROWS, LANE).astype(BF16)
            )

        return fill

    for p in range(NP):
        rows_out(p, mm(HID[...], WD[p]))
    exchange(2, fill_from_scr(os_), os_, orr)

    for p in range(NP):
        XT[p] = X[p].T
    HT[...] = HID[...].T

    arrived(1, gr, 3)
    unpack(gr)

    def to_sibling(k, buf_s, buf_r, s):
        c = pltpu.make_async_remote_copy(
            buf_s, buf_r, sib_ss.at[k, s], sib_rs.at[k, s], device_id=sibling, device_id_type=MESH
        )
        c.start()
        return c

    def to_across(k, buf_s, buf_r):
        c = pltpu.make_async_remote_copy(
            buf_s, buf_r, crs_ss.at[k], crs_rs.at[k], device_id=across, device_id_type=MESH
        )
        c.start()
        return c

    def part_down(p):
        return mm(HT[...], X[p])

    def part_gu(m, p):
        return mm(XT[p], (DG, DU)[m][...])

    sib = {}
    for s in range(2):
        sibd_s[s] = part_down(2 * s + (1 - core)).astype(BF16)
        sib[2, s] = to_sibling(2, sibd_s.at[s], sibd_r.at[s], s)

    def dh_tile(n, carry):
        cols = pl.ds(pl.multiple_of(n * TILE, TILE), TILE)
        dh = mm_last(X[0], WD[0, cols, :])
        for p in range(1, NP):
            dh += mm_last(X[p], WD[p, cols, :])
        DG[:, cols] = (dh * A[:, cols]).astype(BF16)
        DU[:, cols] = (dh * B[:, cols]).astype(BF16)
        return carry

    lax.fori_loop(0, FF // TILE, dh_tile, 0)
    for m in range(2):
        for s in range(2):
            sib_s[m, s] = part_gu(m, 2 * s + (1 - core)).astype(BF16)
            sib[m, s] = to_sibling(m, sib_s.at[m, s], sib_r.at[m, s], s)

    for s in range(2):
        sib[2, s].wait_recv()
    crsd_s[...] = (part_down(crs_dp) + sibd_r[1 - xlo].astype(F32)).astype(BF16)
    crs = [None, None, to_across(2, crsd_s, crsd_r)]
    for m in range(2):
        for s in range(2):
            sib[m, s].wait_recv()
        crs_s[m] = (part_gu(m, crs_dp) + sib_r[m, 1 - xlo].astype(F32)).astype(BF16)
        crs[m] = to_across(m, crs_s.at[m], crs_r.at[m])

    sent(0, xs, 3)
    for p in range(NP):
        rows_out(p, mm_last(DG[...], WG[p]) + mm_last(DU[...], WU[p]))
    exchange(3, fill_from_scr(xs), xs, dxr)

    find[...] = part_down(dp) + sibd_r[xlo].astype(F32)
    for m in range(2):
        fin[m] = part_gu(m, dp) + sib_r[m, xlo].astype(F32)

    arrived(2, orr, 1)
    unpack(orr)
    p0, p1 = onehot(0, 0, S).astype(BF16), onehot(1, 0, S).astype(BF16)
    w0, w1 = column(prb[0, 0:1, :]), column(prb[0, 1:2, :])
    dg0 = jnp.zeros((T, 1), F32)
    dg1 = jnp.zeros((T, 1), F32)
    for p in range(NP):
        cols = slice(p * PC, (p + 1) * PC)
        k0, k1 = mm(p0, X[p]), mm(p1, X[p])
        lay[:, cols] = (w0 * k0 + w1 * k1).astype(BF16)
        c32 = cots[0, :, cols].astype(F32)
        dg0 += jnp.sum(c32 * k0, axis=1, keepdims=True)
        dg1 += jnp.sum(c32 * k1, axis=1, keepdims=True)
    for k, v in enumerate((dg0, dg1)):
        dgate[k : k + 1, :] = jnp.sum(jnp.where(eye, v, 0.0), axis=0, keepdims=True)

    outs = []
    for i, (src, dst) in enumerate(((lay, lay_o), (dgate, dgate_o), (slot_s.at[0], slot_o))):
        outs.append(pltpu.make_async_copy(src, dst, out_sem.at[3 + i]))
        outs[-1].start()
    crs[2].wait_recv()
    crsd_r[...] = (find[...] + crsd_r[...].astype(F32)).astype(BF16)
    outs.append(pltpu.make_async_copy(crsd_r, gd_o, out_sem.at[2]))
    outs[-1].start()
    for m, o in enumerate((gg_o, gu_o)):
        crs[m].wait_recv()
        crs_r[m] = (fin[m] + crs_r[m].astype(F32)).astype(BF16)
        outs.append(pltpu.make_async_copy(crs_r.at[m], o, out_sem.at[m]))
        outs[-1].start()

    arrived(3, dxr, 1)

    sent(1, gs, 3)
    sent(2, os_, 1)
    sent(3, xs, 1)
    for c in near:
        c.wait_send()
    for m in range(3):
        ag[m][0].wait_send()
        ag[m][1].wait_send()
        fwd[m].wait_send()
        crs[m].wait_send()
        for s in range(2):
            sib[m, s].wait_send()
    for o in outs:
        o.wait()


def finish(
    cap,
    slots_in, dxr, lay, dgate, gg, gu, gd,
    dtok_o, lay_o, dgate_o, gg_o, gu_o, gd_o,
    got, dtok, scr, Y, gg_v, gu_v, gd_v, lay_v, dgate_v, slots, gg_w, gu_w, gd_w, got_sem, in_sem, out_sem, dtok_sem, slot_sem,
):
    T, D = dtok.shape
    S, ROWS, _ = got.shape
    NP, _, PC = Y.shape
    step = 16 * cap
    loads = []
    for c in range(S // step):
        rows = pl.ds(c * step, step)
        loads.append(pltpu.make_async_copy(dxr.at[rows], got.at[rows], got_sem.at[c]))
        loads[-1].start()
    slot_load = pltpu.make_async_copy(slots_in, slots, slot_sem)
    slot_load.start()
    through = ((gg, gg_v, gg_o), (gu, gu_v, gu_o), (gd, gd_v, gd_o), (lay, lay_v, lay_o), (dgate, dgate_v, dgate_o))
    wide = (gg_w, gu_w, gd_w)
    copies = []
    for i, (src, held, dst) in enumerate(through):
        copies.append(pltpu.make_async_copy(src, held, in_sem.at[i]))
        copies[-1].start()
    stores = []
    for c in range(S // step):
        loads[c].wait()
        rows = pl.ds(c * step, step)
        scr[pl.ds(0, step * ROWS), :] = got[rows].astype(F32).reshape(step * ROWS, LANE)
        for j in range(ROWS):
            p, o = divmod(j * LANE, PC)
            Y[p, rows, o : o + LANE] = scr[pl.ds(j, step, stride=ROWS), :].astype(BF16)
        while len(stores) < min(2 * c + 1, len(through)):
            i = len(stores)
            copies[i].wait()
            held = through[i][1]
            if i < len(wide):
                wide[i][...] = held[...].astype(F32)
                held = wide[i]
            stores.append(pltpu.make_async_copy(held, through[i][2], out_sem.at[i]))
            stores[-1].start()
    slot_load.wait()
    iota = lax.broadcasted_iota(jnp.int32, (T, S), 1)
    both = jnp.where((slots[:, 0:1] == iota) | (slots[:, 1:2] == iota), 1.0, 0.0).astype(BF16)
    for p in range(NP):
        dtok[:, p * PC : (p + 1) * PC] = mm(both, Y[p]).astype(BF16)
    out = pltpu.make_async_copy(dtok, dtok_o, dtok_sem)
    out.start()
    for c in stores:
        c.wait()
    out.wait()


def on_device(tokens, routes, gate_probs, cotangent, w_gate, w_up, w_down):
    T, D = tokens.shape
    E = lax.axis_size("expert")
    NP = lax.axis_size("dp")
    PC, FF = w_gate.shape[1:]
    cap = max(2, 3 * T * routes.shape[1] // (2 * E))
    S = E * cap
    ROWS = D // LANE
    rows_buf = pltpu.VMEM((S, ROWS, LANE), BF16)
    relay_buf = pltpu.VMEM((S + PLANE * cap, ROWS, LANE), BF16)
    dma = pltpu.SemaphoreType.DMA
    hbm = pl.BlockSpec(memory_space=pl.ANY)
    scratch = [
        pltpu.VMEM((3, T, D), BF16),
        pltpu.VMEM((3, 2, T), jnp.int32),
        pltpu.VMEM((3, 2, T), F32),
        pltpu.VMEM((3, T, D), BF16),
        pltpu.VMEM((T, D), BF16),
        pltpu.VMEM((2, T), F32),
        pltpu.VMEM((3, T, 2), jnp.int32),
        pltpu.VMEM((2 * T, D), BF16),
        *([relay_buf] * 2),
        *([rows_buf] * 4),
        pltpu.VMEM((NP, S, PC), BF16),
        pltpu.VMEM((NP, PC, S), BF16),
        pltpu.VMEM((FF, S), BF16),
        pltpu.VMEM((NP, PC, FF), BF16),
        pltpu.VMEM((NP, PC, FF), BF16),
        pltpu.VMEM((NP, FF, PC), BF16),
        pltpu.VMEM((S, FF), F32),
        pltpu.VMEM((S, FF), F32),
        *([pltpu.VMEM((S, FF), BF16)] * 3),
        pltpu.VMEM((S * ROWS + 8 * ROWS, LANE), F32),
        pltpu.VMEM((2, 2, PC, FF), BF16),
        pltpu.VMEM((2, 2, PC, FF), BF16),
        pltpu.VMEM((2, FF, PC), BF16),
        pltpu.VMEM((2, FF, PC), BF16),
        pltpu.VMEM((2, PC, FF), BF16),
        pltpu.VMEM((2, PC, FF), BF16),
        pltpu.VMEM((FF, PC), BF16),
        pltpu.VMEM((FF, PC), BF16),
        pltpu.VMEM((2, PC, FF), F32),
        pltpu.VMEM((FF, PC), F32),
        dma((4,)), dma((4,)), dma((4,)),
        dma((3,)), dma((6,)), dma((3,)), dma((3,)), dma((3,)), dma((3,)),
        dma((3, 2)), dma((3, 2)), dma((3,)), dma((3,)), dma((4,)), dma((6,)), dma((4, 2)), dma((4, 2)),
    ]
    lay_shape = jax.ShapeDtypeStruct((T, D), BF16)
    dgate_shape = jax.ShapeDtypeStruct((2, T), F32)
    grads = (
        jax.ShapeDtypeStruct((PC, FF), F32),
        jax.ShapeDtypeStruct((PC, FF), F32),
        jax.ShapeDtypeStruct((FF, PC), F32),
    )
    lay, dgate, slots, dxr, gg, gu, gd = pl.pallas_call(
        functools.partial(kernel, cap),
        out_shape=(
            lay_shape,
            dgate_shape,
            jax.ShapeDtypeStruct((T, 2), jnp.int32),
            jax.ShapeDtypeStruct((S, ROWS, LANE), BF16),
            *(jax.ShapeDtypeStruct(g.shape, BF16) for g in grads),
        ),
        in_specs=[hbm] * 7,
        out_specs=(hbm,) * 7,
        scratch_shapes=scratch,
        compiler_params=pltpu.CompilerParams(
            collective_id=0, has_side_effects=True, vmem_limit_bytes=64000 * 1024
        ),
    )(tokens, routes.T, gate_probs.T, cotangent, w_gate[0], w_up[0], w_down[0])
    dtok, lay, dgate, gg, gu, gd = pl.pallas_call(
        functools.partial(finish, cap),
        out_shape=(lay_shape, lay_shape, dgate_shape, *grads),
        in_specs=[hbm] * 7,
        out_specs=(hbm,) * 6,
        scratch_shapes=[
            pltpu.VMEM((S, ROWS, LANE), BF16),
            pltpu.VMEM((T, D), BF16),
            pltpu.VMEM((16 * cap * ROWS + 8 * ROWS, LANE), F32),
            pltpu.VMEM((NP, S, PC), BF16),
            pltpu.VMEM((PC, FF), BF16),
            pltpu.VMEM((PC, FF), BF16),
            pltpu.VMEM((FF, PC), BF16),
            pltpu.VMEM((T, D), BF16),
            pltpu.VMEM((2, T), F32),
            pltpu.VMEM((T, 2), jnp.int32),
            pltpu.VMEM((PC, FF), F32),
            pltpu.VMEM((PC, FF), F32),
            pltpu.VMEM((FF, PC), F32),
            dma((S // (16 * cap),)),
            dma((5,)),
            dma((5,)),
            dma,
            dma,
        ],
        compiler_params=pltpu.CompilerParams(vmem_limit_bytes=64000 * 1024),
    )(slots, dxr, lay, dgate, gg, gu, gd)
    return lay, dtok, dgate.T, gg[None], gu[None], gd[None]


def solution(mesh):
    rows = P(("dp", "expert"), None)
    weights = (P("expert", "dp", None), P("expert", "dp", None), P("expert", None, "dp"))
    return jax.shard_map(
        on_device,
        mesh=mesh,
        in_specs=(rows, rows, rows, rows, *weights),
        out_specs=(rows, rows, rows, *weights),
        check_vma=False,
    )
```
